128 devices in a mesh: bx: 16 (over z, x), bz: 8 (over y, core).
Axes of the slice: x: 4, y: 4, z: 4, core: 2. Of those that a mesh axis runs over, the one named last changes fastest.
Arguments:
- fields: bfloat16 [4, 64, 1024, 4096], P(None, 'bz', None, 'bx'), may hold values from -6 to 6
- breakpoints: int32 [8], replicated, may hold values from 0 to 255, as said below
- tf_color: float32 [8, 3], replicated, may hold values from 0.05 to 1
- tf_opacity: float32 [8], replicated, may hold values from 0.002 to 0.02
- depth_order: int32 [16, 8], replicated, may hold values from 0 to 7, each once within a row
- live_rows: int32 [16, 8, 2], P('bx', 'bz'), may hold values from 0 to 1024, as said below
Outputs:
- image: float32 [4, 1024, 4096], P(None, ('bx', 'bz'))
The draws below stay inside these ranges and needn't reach their ends.
Inputs may be any that keep to these rules, and one draw needn't show every extreme that they name: `breakpoints`: strictly increasing, first 0 and last 255. `live_rows`: for every brick the first row is below 512 and the end row above it; some brick starts at row 0 and some ends at row 1024.
All inputs are finite; a program needn't handle non-finite values.
Results may differ from the reference program's by a relative error of at most 0.0003.
Values may be sent and summed in bfloat16 or wider, within the bound.
No kernel may reach another device: no remote copies, remote signals or barrier semaphores. Data moves between devices by JAX's collectives and lax.ppermute only.
A program may use at most 128 MiB of HBM per device.

```python
import math
import jax
import jax.numpy as jnp
from jax import lax

NF = 4
NBP = 8
BC = 256
Y = 1024
DZ = 8
IW = 4096
DEPTH = 64
N_BX = 16
N_BZ = 8


def draw_breakpoints(key, part):
    inner = jax.random.permutation(jax.random.fold_in(key, 11), 254)[:NBP - 2] + 1
    inner = jnp.sort(inner.astype(jnp.int32))
    return jnp.concatenate([jnp.zeros((1,), jnp.int32), inner, jnp.full((1,), 255, jnp.int32)]).astype(jnp.int32)


def draw_live_rows(key, part):
    first_key, second_key, third_key, fourth_key = jax.random.split(jax.random.fold_in(key, 23), 4)
    count = N_BX * N_BZ
    low = jax.random.randint(first_key, (N_BX, N_BZ), 0, Y // 2).astype(jnp.int32)
    high = (Y - jax.random.randint(second_key, (N_BX, N_BZ), 0, Y // 2)).astype(jnp.int32)
    flat = jnp.arange(count, dtype=jnp.int32).reshape(N_BX, N_BZ)
    chosen_low = jax.random.randint(third_key, (), 0, count).astype(jnp.int32)
    chosen_high = (chosen_low + 1 + jax.random.randint(fourth_key, (), 0, count - 1).astype(jnp.int32)) % count
    low = jnp.where(flat == chosen_low, 0, low)
    high = jnp.where(flat == chosen_high, Y, high)
    return jnp.stack([low, high], axis=-1).astype(jnp.int32)


def block_levels(rng, shape, cuts, smallest, high):
    loudness = 1.0
    for position, parts in cuts:
        steps = jax.random.uniform(jax.random.fold_in(jax.random.fold_in(rng, 6), position), (parts,), jnp.float32, smallest / len(cuts), high / len(cuts))
        loudness = loudness * jnp.repeat(jnp.exp(steps), shape[position] // parts).reshape((-1,) + (1,) * (len(shape) - 1 - position))
    return loudness


def scatter_about(rng, shape, deviation, limit, cuts=(), held_as=jnp.bfloat16):
    result = jax.random.normal(rng, shape, jnp.float32) * deviation
    if len(cuts) > 0:
        result = block_levels(rng, shape, cuts, -0.22, 0.18) * result
    return jnp.clip(result, min=-limit, max=limit).astype(held_as)


def setup_inputs(seed: int = 0) -> dict:
    key_of = jax.random.split(jax.random.key(seed), 7)
    return {
        "fields": scatter_about(key_of[0], (NF, DEPTH, Y, IW), 1.0, 6.0, ((1, 8), (3, 16))),
        "breakpoints": draw_breakpoints(jax.random.fold_in(key_of[6], 71), 0),
        "tf_color": jnp.clip(jax.random.uniform(key_of[2], (NBP, 3), jnp.float32, 0.05, 1.0), 0.05, 1.0),
        "tf_opacity": jnp.clip(jnp.exp(jax.random.uniform(key_of[3], (NBP,), jnp.float32, math.log(0.002), math.log(0.02))), 0.002, 0.02),
        "depth_order": jax.vmap(lambda own: jax.random.permutation(own, N_BZ))(jax.random.split(key_of[4], N_BX)).reshape((N_BX, N_BZ)).astype(jnp.int32),
        "live_rows": draw_live_rows(jax.random.fold_in(key_of[6], 71), 0),
    }


def classify(raw, breakpoints, tf_color, tf_opacity):
    level = 255.0 * jax.nn.sigmoid(raw[0])
    swirl = raw[1] * raw[1] + raw[2] * raw[2] + raw[3] * raw[3]
    marks = breakpoints.astype(jnp.float32)
    ramps = []
    for j in range(1, NBP):
        ramps.append(jnp.clip((level - marks[j - 1]) / (marks[j] - marks[j - 1]), 0.0, 1.0))

    def lookup(values):
        total = values[0] + jnp.zeros_like(level)
        for j in range(1, NBP):
            total = total + (values[j] - values[j - 1]) * ramps[j - 1]
        return total

    alpha = 1.0 - jnp.exp(-lookup(tf_opacity) * (0.25 + swirl))
    return jnp.stack([alpha * lookup(tf_color[:, 0]), alpha * lookup(tf_color[:, 1]), alpha * lookup(tf_color[:, 2]), alpha])


def reference(fields, breakpoints, tf_color, tf_opacity, depth_order, live_rows):
    reach = 3 * (DEPTH - 1) // 8 + 1
    rows = jnp.arange(Y, dtype=jnp.int32)
    partials = []
    for brick in range(N_BZ):
        def advance(k, acc):
            zglobal = (brick * DZ + k).astype(jnp.int32)
            raw = lax.dynamic_index_in_dim(fields, zglobal, 1, keepdims=False).astype(jnp.float32)
            sample = classify(raw, breakpoints, tf_color, tf_opacity)
            padded = jnp.pad(sample, ((0, 0), (0, 0), (reach, 0)))
            whole = (3 * zglobal) // 8
            frac = ((3 * zglobal) % 8).astype(jnp.float32) / 8.0
            near = lax.dynamic_slice_in_dim(padded, reach - whole, IW, 2)
            far = lax.dynamic_slice_in_dim(padded, reach - whole - 1, IW, 2)
            sheared = (1.0 - frac) * near + frac * far
            return acc + (1.0 - acc[3:4]) * sheared

        acc = lax.fori_loop(0, DZ, advance, jnp.zeros((4, Y, IW), jnp.float32))
        low = live_rows[:, brick, 0]
        high = live_rows[:, brick, 1]
        keep = ((rows[:, None] >= low[None, :]) & (rows[:, None] < high[None, :])).astype(jnp.float32)
        keep = jnp.repeat(keep, BC, axis=1)
        partials.append(acc * keep[None])
    stacked = jnp.stack(partials).reshape(N_BZ, 4, Y, N_BX, BC)
    slots = jnp.arange(N_BZ, dtype=jnp.int32)
    image = jnp.zeros((4, Y, N_BX, BC), jnp.float32)
    for k in range(N_BZ):
        pick = (depth_order[:, k][:, None] == slots[None, :]).astype(jnp.float32)
        chosen = jnp.zeros((4, Y, N_BX, BC), jnp.float32)
        for zslot in range(N_BZ):
            chosen = chosen + stacked[zslot] * pick[:, zslot][None, None, :, None]
        image = image + (1.0 - image[3:4]) * chosen
    return image.reshape(4, Y, IW)
```

```python
import functools

import jax
import jax.numpy as jnp
from jax import lax
from jax.experimental import pallas as pl
from jax.experimental.pallas import tpu as pltpu
from jax.sharding import PartitionSpec as P

NBP = 8
LANES = 128
TILE = 8
BLOCK = 128
HALF = BLOCK // 2
CODE = 65534.0
LOG2E = 1.4426950408889634
LOOKUP = "gather"


def tables(bp_ref, color_ref, opacity_ref):
    marks = [bp_ref[j].astype(jnp.float32) * (1.0 / 127.5) - 1.0 for j in range(NBP)]
    values = [[color_ref[j, c] for j in range(NBP)] for c in range(3)]
    values.append([opacity_ref[j] for j in range(NBP)])
    row = lax.broadcasted_iota(jnp.int32, (TILE, LANES), 0)

    def by_segment(scalars):
        table = jnp.full((TILE, LANES), scalars[0], jnp.float32)
        for j in range(1, NBP - 1):
            table = jnp.where(row >= j, scalars[j], table)
        return table

    low = by_segment(marks[: NBP - 1])
    width = by_segment(marks[1:]) - low
    pairs = []
    for c, value in enumerate(values):
        start = by_segment(value[: NBP - 1])
        slope = (by_segment(value[1:]) - start) / width
        offset = start - slope * low
        if c == 3:
            slope, offset = -LOG2E * slope, -LOG2E * offset
        pairs.append((offset, slope))
    return marks, pairs


def classify(raw, marks, pairs):
    h = jnp.tanh(raw[0] * 0.5)
    swirl = raw[1] * raw[1] + raw[2] * raw[2] + (raw[3] * raw[3] + 0.25)
    index = jnp.zeros(h.shape, jnp.int32)
    for j in range(1, NBP - 1):
        index = jnp.where(h >= marks[j], j, index)
    looked = []
    for offset, slope in pairs:
        parts = []
        for r in range(0, h.shape[0], TILE):
            own = index[r : r + TILE]
            parts.append(
                jnp.take_along_axis(offset, own, axis=0, mode="promise_in_bounds")
                + jnp.take_along_axis(slope, own, axis=0, mode="promise_in_bounds") * h[r : r + TILE]
            )
        looked.append(parts[0] if len(parts) == 1 else jnp.concatenate(parts, axis=0))
    return looked[:3], jnp.exp2(looked[3] * swirl)


def steps(slices):
    return [(3 * k // 8, (3 * k % 8) / 8.0) for k in range(slices)]


def encode(value):
    return (jnp.sqrt(value) * CODE + 0.5).astype(jnp.int32) - 32767


def boundary(halo_ref, own_ref, keep, marks, pairs, slices, edge_ref):
    lane = lax.broadcasted_iota(jnp.int32, (HALF, LANES), 1)
    slot = lax.rem(lane, 8)
    slab = lax.rem(lax.div(lane, 8), 8)
    raw = []
    for f in range(4):
        raw.append(jnp.where(slot < 3, halo_ref[f].astype(jnp.float32), own_ref[f].astype(jnp.float32)))
    color, through = classify(raw, marks, pairs)
    if keep is not None:
        through = jnp.where((slot < 3) & (keep == 0), 1.0, through)
    alpha = 1.0 - through
    samples = [alpha * c for c in color] + [through]
    whole = lax.div(3 * slab, 8)
    frac = lax.rem(3 * slab, 8).astype(jnp.float32) * 0.125
    sheared = [jnp.zeros((HALF, LANES), jnp.float32)] * 4
    for s in range(steps(slices)[-1][0] + 2):
        weight = jnp.where(whole == s, 1.0 - frac, 0.0) + jnp.where(whole + 1 == s, frac, 0.0)
        for c in range(4):
            moved = samples[c] if s == 0 else pltpu.roll(samples[c], s, 1)
            sheared[c] = sheared[c] + weight * moved
    product = sheared[3]
    for s in (1, 2, 4):
        product = product * jnp.where(slab >= s, pltpu.roll(product, 8 * s, 1), 1.0)
    before = jnp.where(slab >= 1, pltpu.roll(product, 8, 1), 1.0)
    for c in range(3):
        total = before * sheared[c]
        for s in (1, 2, 4):
            total = total + jnp.where(slab >= s, pltpu.roll(total, 8 * s, 1), 0.0)
        edge_ref[c] = total
    edge_ref[3] = 1.0 - product


def brick_kernel(slices, right, bp_ref, color_ref, opacity_ref, place_ref, fields_ref, halo_ref, own_ref, out_ref, edge_ref):
    marks, pairs = tables(bp_ref, color_ref, opacity_ref)
    boundary(halo_ref, own_ref, None if right else place_ref[0], marks, pairs, slices, edge_ref)
    plan = steps(slices)
    first = pl.program_id(0) * BLOCK
    rows = 2 * TILE

    def group(j, carry):
        base = pl.multiple_of(j * rows, rows)
        acc = [jnp.zeros((rows, LANES), jnp.float32) for _ in range(3)]
        far = [jnp.zeros((rows, LANES), jnp.float32) for _ in range(3)]
        through = jnp.ones((rows, LANES), jnp.float32)
        at = 0
        for k in range(slices):
            whole, frac = plan[k]
            if whole != at:
                acc = [pltpu.roll(a, LANES - (whole - at), 1) for a in acc]
                far = [pltpu.roll(a, LANES - (whole - at), 1) for a in far]
                through = pltpu.roll(through, LANES - (whole - at), 1)
                at = whole
            raw = [fields_ref[f, k, pl.ds(base, rows), :].astype(jnp.float32) for f in range(4)]
            color, clear = classify(raw, marks, pairs)
            alpha = 1.0 - clear
            near_t = through * (1.0 - frac) if frac else through
            near_w = near_t * alpha
            acc = [a + near_w * c for a, c in zip(acc, color)]
            if frac:
                far_t = through * frac
                far_w = pltpu.roll(far_t, LANES - 1, 1) * alpha
                far = [a + far_w * c for a, c in zip(far, color)]
                through = near_t * clear + far_t * pltpu.roll(clear, 1, 1)
            else:
                through = near_t * clear
        back = at
        done = [pltpu.roll(a + pltpu.roll(b, 1, 1), back, 1) for a, b in zip(acc, far)]
        done.append(1.0 - pltpu.roll(through, back, 1))
        lane = lax.broadcasted_iota(jnp.int32, (TILE, LANES), 1)
        for r in range(2):
            tile = 2 * j + r
            side = lax.div(tile, HALF // TILE)
            spot = pl.multiple_of((tile - side * (HALF // TILE)) * TILE, TILE)
            turn = lax.rem(LANES + LANES - (64 * side + 8 * (slices - 1) + 3), LANES)
            row = lax.broadcasted_iota(jnp.int32, (TILE, LANES), 0) + (first + tile * TILE)
            low, high = place_ref[1], place_ref[2]
            if right:
                inside = lane < place_ref[5]
                low = jnp.where(inside, low, place_ref[3])
                high = jnp.where(inside, high, place_ref[4])
            live = (row >= low) & (row < high)
            codes = []
            for c in range(4):
                value = done[c][r * TILE : (r + 1) * TILE]
                edge = pltpu.roll(edge_ref[c, pl.ds(spot, TILE), :], turn, 1)
                value = jnp.where(lane < 3, edge, value)
                value = jnp.where(live, jnp.maximum(value, 0.0), 0.0)
                codes.append(encode(value))
            out_ref[tile] = jnp.concatenate(codes, axis=0).astype(jnp.int16)
        return carry

    lax.fori_loop(0, BLOCK // rows, group, 0)


def brick_half(right, breakpoints, tf_color, tf_opacity, place, fields, halo, own):
    slices, height = fields.shape[1], fields.shape[2]
    half = 1 if right else 0
    smem = pl.BlockSpec(memory_space=pltpu.SMEM)
    compact = pl.BlockSpec((4, HALF, LANES), lambda i: (0, i, 0))
    return pl.pallas_call(
        functools.partial(brick_kernel, slices, right),
        grid=(height // BLOCK,),
        in_specs=[smem, smem, smem, smem, pl.BlockSpec((4, slices, BLOCK, LANES), lambda i: (0, 0, i, half)), compact, compact],
        out_specs=pl.BlockSpec((BLOCK // TILE, 4 * TILE, LANES), lambda i: (i, 0, 0)),
        out_shape=jax.ShapeDtypeStruct((height // TILE, 4 * TILE, LANES), jnp.int16),
        scratch_shapes=[pltpu.VMEM((4, HALF, LANES), jnp.float32)],
        compiler_params=pltpu.CompilerParams(vmem_limit_bytes=40 * 1024 * 1024),
        cost_estimate=pl.CostEstimate(flops=60 * slices * height * LANES, bytes_accessed=8 * slices * height * LANES, transcendentals=0),
        name="brick_right" if right else "brick_left",
    )(breakpoints, tf_color, tf_opacity, place, fields, halo, own)


def rim_kernel(slices, fields_ref, left_ref, right_ref):
    lane = lax.broadcasted_iota(jnp.int32, (2 * TILE, LANES), 1)
    rows = 2 * TILE

    def group(j, carry):
        base = pl.multiple_of(j * rows, rows)
        for f in range(4):
            for half, ref in ((0, left_ref), (1, right_ref)):
                total = jnp.zeros((rows, LANES), jnp.float32)
                for g in range(2):
                    for k in range(slices):
                        begin = g * 64 + k * 8
                        x = fields_ref[f, k, pl.ds(base + g * HALF, rows), half * LANES : (half + 1) * LANES]
                        x = pltpu.roll(x.astype(jnp.float32), (begin + 3) % LANES, 1)
                        total = jnp.where((lane >= begin) & (lane < begin + 8), x, total)
                ref[f, pl.ds(base, rows), :] = total.astype(ref.dtype)
        return carry

    lax.fori_loop(0, HALF // rows, group, 0)


def rims(fields):
    _, slices, height, width = fields.shape
    compact = pl.BlockSpec((4, HALF, LANES), lambda i: (0, i, 0))
    shape = jax.ShapeDtypeStruct((4, height // 2, LANES), jnp.bfloat16)
    return pl.pallas_call(
        functools.partial(rim_kernel, slices),
        grid=(height // BLOCK,),
        in_specs=[pl.BlockSpec((4, slices, BLOCK, width), lambda i: (0, 0, i, 0))],
        out_specs=[compact, compact],
        out_shape=[shape, shape],
        compiler_params=pltpu.CompilerParams(vmem_limit_bytes=40 * 1024 * 1024),
        cost_estimate=pl.CostEstimate(flops=4 * slices * height * width, bytes_accessed=8 * slices * height * width, transcendentals=0),
        name="rims",
    )(fields)


def image_kernel(count_x, count_z, order_ref, left_ref, right_ref, out_ref):
    lane = lax.broadcasted_iota(jnp.int32, (4 * TILE, LANES), 1)

    def decode(code):
        root = (code.astype(jnp.int32) + 32767).astype(jnp.float32) * (1.0 / CODE)
        return root * root

    def column(i, carry):
        image = [jnp.zeros((3 * TILE, LANES), jnp.float32) for _ in range(2)]
        through = [jnp.ones((TILE, LANES), jnp.float32) for _ in range(2)]
        for k in range(count_z):
            d = order_ref[i, k]
            turn = 3 * d
            own = i * count_z + d
            behind = jnp.maximum(i - 1, 0) * count_z + d
            left = pltpu.roll(decode(left_ref[own]), turn, 1)
            right = pltpu.roll(decode(right_ref[own]), turn, 1)
            before = jnp.where(i > 0, pltpu.roll(decode(right_ref[behind]), turn, 1), 0.0)
            pieces = (jnp.where(lane < turn, before, left), jnp.where(lane < turn, left, right))
            for side in range(2):
                piece = pieces[side]
                t = through[side]
                image[side] = image[side] + jnp.concatenate([t, t, t], axis=0) * piece[: 3 * TILE]
                through[side] = t * (1.0 - piece[3 * TILE :])
        for side in range(2):
            at = pl.multiple_of((2 * i + side) * LANES, LANES)
            for c in range(3):
                out_ref[c, :, pl.ds(at, LANES)] = image[side][c * TILE : (c + 1) * TILE]
            out_ref[3, :, pl.ds(at, LANES)] = 1.0 - through[side]
        return carry

    lax.fori_loop(0, count_x, column, 0)


def compose(order, left, right, count_x, count_z):
    vmem = pl.BlockSpec(memory_space=pltpu.VMEM)
    return pl.pallas_call(
        functools.partial(image_kernel, count_x, count_z),
        in_specs=[pl.BlockSpec(memory_space=pltpu.SMEM), vmem, vmem],
        out_specs=vmem,
        out_shape=jax.ShapeDtypeStruct((4, TILE, count_x * 2 * LANES), jnp.float32),
        compiler_params=pltpu.CompilerParams(vmem_limit_bytes=40 * 1024 * 1024),
        name="compose",
    )(order, left, right)


def per_device(fields, breakpoints, tf_color, tf_opacity, depth_order, live_rows):
    count_x, count_z = lax.axis_size("bx"), lax.axis_size("bz")
    here, depth = lax.axis_index("bx"), lax.axis_index("bz")
    live = live_rows.reshape(2)
    next_live = lax.ppermute(live, "bx", [(i + 1, i) for i in range(count_x - 1)])
    scalars = jnp.stack([(here > 0).astype(jnp.int32), live[0], live[1], next_live[0], next_live[1], LANES - 3 * depth])
    left_rim, right_rim = rims(fields)
    behind = lax.ppermute(right_rim, "bx", [(i, i + 1) for i in range(count_x - 1)])
    tf = (breakpoints, tf_color, tf_opacity, scalars)
    right = brick_half(True, *tf, fields, left_rim, right_rim)
    right = lax.all_to_all(right, ("bx", "bz"), split_axis=0, concat_axis=0, tiled=True)
    left = brick_half(False, *tf, fields, behind, left_rim)
    left = lax.all_to_all(left, ("bx", "bz"), split_axis=0, concat_axis=0, tiled=True)
    return compose(depth_order, left, right, count_x, count_z)


def solution(mesh):
    return jax.shard_map(
        per_device,
        mesh=mesh,
        in_specs=(P(None, "bz", None, "bx"), P(), P(), P(), P(), P("bx", "bz", None)),
        out_specs=P(None, ("bx", "bz"), None),
        check_vma=False,
    )
```

```python
import functools

import jax
import jax.numpy as jnp
from jax import lax
from jax.experimental import pallas as pl
from jax.experimental.pallas import tpu as pltpu
from jax.sharding import PartitionSpec as P

NBP = 8
LANES = 128
TILE = 8
BLOCK = 256
HALF = BLOCK // 2
GROUP = 16
UNROLL = 2
CODE = 65534.0
LOG2E = 1.4426950408889634
LOOKUP = "gather"


def tables(bp_ref, color_ref, opacity_ref):
    marks = [bp_ref[j].astype(jnp.float32) * (1.0 / 127.5) - 1.0 for j in range(NBP)]
    values = [[color_ref[j, c] for j in range(NBP)] for c in range(3)]
    values.append([opacity_ref[j] for j in range(NBP)])
    row = lax.broadcasted_iota(jnp.int32, (TILE, LANES), 0)

    def by_segment(scalars):
        table = jnp.full((TILE, LANES), scalars[0], jnp.float32)
        for j in range(1, NBP - 1):
            table = jnp.where(row >= j, scalars[j], table)
        return table

    low = by_segment(marks[: NBP - 1])
    width = by_segment(marks[1:]) - low
    pairs = []
    for c, value in enumerate(values):
        start = by_segment(value[: NBP - 1])
        slope = (by_segment(value[1:]) - start) / width
        offset = start - slope * low
        if c == 3:
            slope, offset = -LOG2E * slope, -LOG2E * offset
        pairs.append((offset, slope))
    return marks, pairs


def classify(raw, marks, pairs):
    h = jnp.tanh(raw[0] * 0.5)
    swirl = raw[1] * raw[1] + raw[2] * raw[2] + (raw[3] * raw[3] + 0.25)
    index = jnp.zeros(h.shape, jnp.int32)
    for j in range(1, NBP - 1):
        index = jnp.where(h >= marks[j], j, index)
    looked = []
    for offset, slope in pairs:
        parts = []
        for r in range(0, h.shape[0], TILE):
            own = index[r : r + TILE]
            parts.append(
                jnp.take_along_axis(offset, own, axis=0, mode="promise_in_bounds")
                + jnp.take_along_axis(slope, own, axis=0, mode="promise_in_bounds") * h[r : r + TILE]
            )
        looked.append(parts[0] if len(parts) == 1 else jnp.concatenate(parts, axis=0))
    return looked[:3], jnp.exp2(looked[3] * swirl)


def steps(slices):
    return [(3 * k // 8, (3 * k % 8) / 8.0) for k in range(slices)]


def turned(pair, columns):
    if columns == 0:
        return pair
    moved = [pltpu.roll(p, columns % LANES, 1) for p in pair]
    lane = lax.broadcasted_iota(jnp.int32, pair[0].shape, 1)
    if columns > 0:
        return [moved[0], jnp.where(lane < columns, moved[0], moved[1])]
    return [jnp.where(lane >= LANES + columns, moved[1], moved[0]), moved[1]]


def encode(value):
    return (jnp.sqrt(value) * CODE + 0.5).astype(jnp.int32) - 32767


def boundary(halo_ref, own_ref, keep, marks, pairs, slices):
    lane = lax.broadcasted_iota(jnp.int32, (HALF, LANES), 1)
    slot = lax.rem(lane, 8)
    slab = lax.rem(lax.div(lane, 8), 8)
    raw = []
    for f in range(4):
        raw.append(jnp.where(slot < 3, halo_ref[f].astype(jnp.float32), own_ref[f].astype(jnp.float32)))
    color, through = classify(raw, marks, pairs)
    through = jnp.where((slot < 3) & (keep == 0), 1.0, through)
    alpha = 1.0 - through
    samples = [alpha * c for c in color] + [through]
    whole = lax.div(3 * slab, 8)
    frac = lax.rem(3 * slab, 8).astype(jnp.float32) * 0.125
    sheared = [jnp.zeros((HALF, LANES), jnp.float32)] * 4
    for s in range(steps(slices)[-1][0] + 2):
        weight = jnp.where(whole == s, 1.0 - frac, 0.0) + jnp.where(whole + 1 == s, frac, 0.0)
        for c in range(4):
            moved = samples[c] if s == 0 else pltpu.roll(samples[c], s, 1)
            sheared[c] = sheared[c] + weight * moved
    product = sheared[3]
    for s in (1, 2, 4):
        product = product * jnp.where(slab >= s, pltpu.roll(product, 8 * s, 1), 1.0)
    before = jnp.where(slab >= 1, pltpu.roll(product, 8, 1), 1.0)
    result = []
    for c in range(3):
        total = before * sheared[c]
        for s in (1, 2, 4):
            total = total + jnp.where(slab >= s, pltpu.roll(total, 8 * s, 1), 0.0)
        result.append(total)
    return result + [1.0 - product]


def edge_kernel(slices, bp_ref, color_ref, opacity_ref, place_ref, halo_ref, own_ref, codes_ref, out_ref, edge_ref):
    marks, pairs = tables(bp_ref, color_ref, opacity_ref)
    lane = lax.broadcasted_iota(jnp.int32, (HALF, LANES), 1)
    row = lax.broadcasted_iota(jnp.int32, (HALF, LANES), 0) + pl.program_id(0) * BLOCK + jnp.where(lane < 64, 0, HALF)
    live = (row >= place_ref[1]) & (row < place_ref[2])
    for c, value in enumerate(boundary(halo_ref, own_ref, place_ref[0], marks, pairs, slices)):
        edge_ref[c] = encode(jnp.where(live, jnp.maximum(value, 0.0), 0.0))
    lane = lax.broadcasted_iota(jnp.int32, (4 * TILE, LANES), 1)
    for g in range(2):
        turn = (2 * LANES - (64 * g + 8 * (slices - 1) + 3)) % LANES
        for t in range(HALF // TILE):
            tile = g * (HALF // TILE) + t
            edge = jnp.concatenate([edge_ref[c, t * TILE : (t + 1) * TILE, :] for c in range(4)], axis=0)
            codes = jnp.where(lane < 3, pltpu.roll(edge, turn, 1), codes_ref[tile].astype(jnp.int32))
            out_ref[tile] = codes.astype(jnp.int16)


def with_edges(slices, breakpoints, tf_color, tf_opacity, place, halo, own, codes):
    smem = pl.BlockSpec(memory_space=pltpu.SMEM)
    compact = pl.BlockSpec((4, HALF, LANES), lambda i: (0, i, 0))
    first = pl.BlockSpec((BLOCK // TILE, 4 * TILE, LANES), lambda i: (i, 0, 0))
    return pl.pallas_call(
        functools.partial(edge_kernel, slices),
        grid=(codes.shape[0] * TILE // BLOCK,),
        in_specs=[smem, smem, smem, smem, compact, compact, first],
        out_specs=first,
        out_shape=jax.ShapeDtypeStruct(codes.shape, codes.dtype),
        scratch_shapes=[pltpu.VMEM((4, HALF, LANES), jnp.int32)],
        input_output_aliases={6: 0},
        compiler_params=pltpu.CompilerParams(vmem_limit_bytes=40 * 1024 * 1024),
        name="edges",
    )(breakpoints, tf_color, tf_opacity, place, halo, own, codes)


def brick_kernel(slices, bp_ref, color_ref, opacity_ref, place_ref, fields_ref, out_ref):
    marks, pairs = tables(bp_ref, color_ref, opacity_ref)
    plan = steps(slices)
    first = pl.program_id(0) * BLOCK
    rows = GROUP

    def group(j, carry):
        base = pl.multiple_of(j * rows, rows)
        sums = {}

        def add(s, weight, color):
            for c in range(3):
                terms = [w * q[c] for w, q in zip(weight, color)]
                sums[s, c] = [p + q for p, q in zip(sums[s, c], terms)] if (s, c) in sums else terms

        through = None
        for k in range(slices):
            whole, frac = plan[k]
            color, clear = [], []
            for side in range(2):
                raw = [
                    fields_ref[f, k, pl.ds(base, rows), side * LANES : (side + 1) * LANES].astype(jnp.float32) for f in range(4)
                ]
                some, clean = classify(raw, marks, pairs)
                color.append(some)
                clear.append(clean)
            alpha = [1.0 - c for c in clear]
            if through is None:
                add(0, alpha, color)
                through = clear
                continue
            near = [t * (1.0 - frac) for t in through] if frac else through
            add(whole, [w * a for w, a in zip(turned(near, -whole), alpha)], color)
            after = [n * c for n, c in zip(near, turned(clear, whole))]
            if frac:
                far = [t * frac for t in through]
                add(whole + 1, [w * a for w, a in zip(turned(far, -whole - 1), alpha)], color)
                after = [p + n * c for p, n, c in zip(after, far, turned(clear, whole + 1))]
            through = after
        reach = plan[-1][0] + 2
        done = []
        for c in range(3):
            moved = [turned(sums[s, c], s) for s in range(reach)]
            done.append([sum(m[side] for m in moved) for side in range(2)])
        done.append([1.0 - t for t in through])
        lane = lax.broadcasted_iota(jnp.int32, (TILE, LANES), 1)
        for r in range(rows // TILE):
            tile = (rows // TILE) * j + r
            row = lax.broadcasted_iota(jnp.int32, (TILE, LANES), 0) + (first + tile * TILE)
            live = [(row >= place_ref[1]) & (row < place_ref[2])]
            inside = lane < place_ref[5]
            live.append((row >= jnp.where(inside, place_ref[1], place_ref[3])) & (row < jnp.where(inside, place_ref[2], place_ref[4])))
            for side in range(2):
                codes = []
                for c in range(4):
                    value = done[c][side][r * TILE : (r + 1) * TILE]
                    codes.append(encode(jnp.where(live[side], jnp.maximum(value, 0.0), 0.0)))
                out_ref[tile, :, side * LANES : (side + 1) * LANES] = jnp.concatenate(codes, axis=0).astype(jnp.int16)
        return carry

    lax.fori_loop(0, BLOCK // rows, group, 0, unroll=UNROLL)


def brick(breakpoints, tf_color, tf_opacity, place, fields):
    _, slices, height, width = fields.shape
    smem = pl.BlockSpec(memory_space=pltpu.SMEM)
    return pl.pallas_call(
        functools.partial(brick_kernel, slices),
        grid=(height // BLOCK,),
        in_specs=[smem, smem, smem, smem, pl.BlockSpec((4, slices, BLOCK, width), lambda i: (0, 0, i, 0))],
        out_specs=pl.BlockSpec((BLOCK // TILE, 4 * TILE, width), lambda i: (i, 0, 0)),
        out_shape=jax.ShapeDtypeStruct((height // TILE, 4 * TILE, width), jnp.int16),
        compiler_params=pltpu.CompilerParams(vmem_limit_bytes=40 * 1024 * 1024),
        cost_estimate=pl.CostEstimate(flops=60 * slices * height * width, bytes_accessed=8 * slices * height * width, transcendentals=0),
        name="brick",
    )(breakpoints, tf_color, tf_opacity, place, fields)


def rim_kernel(slices, fields_ref, rim_ref):
    rows = 2 * TILE
    lane = lax.broadcasted_iota(jnp.int32, (rows, LANES), 1)

    def group(j, carry):
        base = pl.multiple_of(j * rows, rows)
        for f in range(4):
            total = jnp.zeros((rows, LANES), jnp.float32)
            for g in range(2):
                for k in range(slices):
                    begin = g * 64 + k * 8
                    left = fields_ref[f, k, pl.ds(base + g * HALF, rows), :LANES].astype(jnp.float32)
                    right = fields_ref[f, k, pl.ds(base + g * HALF, rows), LANES:].astype(jnp.float32)
                    both = pltpu.roll(jnp.where(lane < 64, left, right), (begin + 3) % LANES, 1)
                    total = jnp.where((lane >= begin) & (lane < begin + 8), both, total)
            rim_ref[f, pl.ds(base, rows), :] = total.astype(rim_ref.dtype)
        return carry

    lax.fori_loop(0, HALF // rows, group, 0)


def rims(fields):
    _, slices, height, width = fields.shape
    compact = pl.BlockSpec((4, HALF, LANES), lambda i: (0, i, 0))
    return pl.pallas_call(
        functools.partial(rim_kernel, slices),
        grid=(height // BLOCK,),
        in_specs=[pl.BlockSpec((4, slices, BLOCK, width), lambda i: (0, 0, i, 0))],
        out_specs=compact,
        out_shape=jax.ShapeDtypeStruct((4, height // 2, LANES), jnp.bfloat16),
        compiler_params=pltpu.CompilerParams(vmem_limit_bytes=40 * 1024 * 1024),
        cost_estimate=pl.CostEstimate(flops=4 * slices * height * width, bytes_accessed=8 * slices * height * width, transcendentals=0),
        name="rims",
    )(fields)


def image_kernel(count_x, count_z, order_ref, codes_ref, out_ref):
    lane = lax.broadcasted_iota(jnp.int32, (4 * TILE, LANES), 1)

    def decode(code):
        root = (code.astype(jnp.int32) + 32767).astype(jnp.float32) * (1.0 / CODE)
        return root * root

    def column(i, carry):
        image = [jnp.zeros((3 * TILE, LANES), jnp.float32) for _ in range(2)]
        through = [jnp.ones((TILE, LANES), jnp.float32) for _ in range(2)]
        for k in range(count_z):
            d = order_ref[i, k]
            turn = 3 * d
            own = i * count_z + d
            behind = jnp.maximum(i - 1, 0) * count_z + d
            left = pltpu.roll(decode(codes_ref[own, :, :LANES]), turn, 1)
            right = pltpu.roll(decode(codes_ref[own, :, LANES:]), turn, 1)
            before = jnp.where(i > 0, pltpu.roll(decode(codes_ref[behind, :, LANES:]), turn, 1), 0.0)
            pieces = (jnp.where(lane < turn, before, left), jnp.where(lane < turn, left, right))
            for side in range(2):
                piece = pieces[side]
                t = through[side]
                image[side] = image[side] + jnp.concatenate([t, t, t], axis=0) * piece[: 3 * TILE]
                through[side] = t * (1.0 - piece[3 * TILE :])
        for side in range(2):
            at = pl.multiple_of((2 * i + side) * LANES, LANES)
            for c in range(3):
                out_ref[c, :, pl.ds(at, LANES)] = image[side][c * TILE : (c + 1) * TILE]
            out_ref[3, :, pl.ds(at, LANES)] = 1.0 - through[side]
        return carry

    lax.fori_loop(0, count_x, column, 0)


def compose(order, codes, count_x, count_z):
    vmem = pl.BlockSpec(memory_space=pltpu.VMEM)
    return pl.pallas_call(
        functools.partial(image_kernel, count_x, count_z),
        in_specs=[pl.BlockSpec(memory_space=pltpu.SMEM), vmem],
        out_specs=vmem,
        out_shape=jax.ShapeDtypeStruct((4, TILE, count_x * 2 * LANES), jnp.float32),
        compiler_params=pltpu.CompilerParams(vmem_limit_bytes=40 * 1024 * 1024),
        name="compose",
    )(order, codes)


def per_device(fields, breakpoints, tf_color, tf_opacity, depth_order, live_rows):
    count_x, count_z = lax.axis_size("bx"), lax.axis_size("bz")
    here, depth = lax.axis_index("bx"), lax.axis_index("bz")
    live = live_rows.reshape(2)
    next_live = lax.ppermute(live, "bx", [(i + 1, i) for i in range(count_x - 1)])
    scalars = jnp.stack([(here > 0).astype(jnp.int32), live[0], live[1], next_live[0], next_live[1], LANES - 3 * depth])
    rim = rims(fields)
    behind = lax.ppermute(rim, "bx", [(i, i + 1) for i in range(count_x - 1)])
    tf = (breakpoints, tf_color, tf_opacity, scalars)
    codes = with_edges(fields.shape[1], *tf, behind, rim, brick(*tf, fields))
    codes = lax.all_to_all(codes, ("bx", "bz"), split_axis=0, concat_axis=0, tiled=True)
    return compose(depth_order, codes, count_x, count_z)


def solution(mesh):
    return jax.shard_map(
        per_device,
        mesh=mesh,
        in_specs=(P(None, "bz", None, "bx"), P(), P(), P(), P(), P("bx", "bz", None)),
        out_specs=P(None, ("bx", "bz"), None),
        check_vma=False,
    )
```

```python
import functools

import jax
import jax.numpy as jnp
from jax import lax
from jax.experimental import pallas as pl
from jax.experimental.pallas import tpu as pltpu
from jax.sharding import PartitionSpec as P

NBP = 8
LANES = 128
TILE = 8
BLOCK = 128
HALF = BLOCK // 2
GROUP = 16
SUB = GROUP // 2
UNROLL = 2
EDGES = 512
COLUMNS = 1
PATCH = 4
DEPTHS = 8
CODE = 32767.0
LOG2E = 1.4426950408889634


def tables(bp_ref, color_ref, opacity_ref):
    marks = [bp_ref[j].astype(jnp.float32) * (1.0 / 127.5) - 1.0 for j in range(NBP)]
    values = [[color_ref[j, c] for j in range(NBP)] for c in range(3)]
    values.append([opacity_ref[j] for j in range(NBP)])
    row = lax.broadcasted_iota(jnp.int32, (TILE, LANES), 0)

    def by_segment(scalars):
        table = jnp.full((TILE, LANES), scalars[0], jnp.float32)
        for j in range(1, NBP - 1):
            table = jnp.where(row >= j, scalars[j], table)
        return table

    low = by_segment(marks[: NBP - 1])
    width = by_segment(marks[1:]) - low
    pairs = []
    for c, value in enumerate(values):
        if c < 3:
            value = [v * (CODE * CODE) for v in value]
        start = by_segment(value[: NBP - 1])
        slope = (by_segment(value[1:]) - start) / width
        offset = start - slope * low
        if c == 3:
            slope, offset = -LOG2E * slope, -LOG2E * offset
        pairs.append((offset, slope))
    return marks, (by_segment(marks[1 : NBP - 1] + [2.0]), pairs)


def looked_up(table, index):
    return jnp.take_along_axis(table, index, axis=0, mode="promise_in_bounds")


def classify(raw, marks, pairs):
    h = jnp.tanh(raw[0] * 0.5)
    swirl = raw[1] * raw[1] + raw[2] * raw[2] + (raw[3] * raw[3] + 0.25)
    index = jnp.zeros(h.shape, jnp.int32)
    for j in range(2, NBP - 1, 2):
        index = jnp.where(h >= marks[j], j, index)
    between, pairs = pairs
    parts = []
    for r in range(0, h.shape[0], TILE):
        segment, level = index[r : r + TILE], h[r : r + TILE]
        segment = jnp.where(level >= looked_up(between, segment), segment + 1, segment)
        parts.append([looked_up(offset, segment) + looked_up(slope, segment) * level for offset, slope in pairs])
    looked = [p[0] if len(p) == 1 else jnp.concatenate(p, axis=0) for p in zip(*parts)]
    return looked[:3], jnp.exp2(looked[3] * swirl)


def steps(slices):
    return [(3 * k // 8, (3 * k % 8) / 8.0) for k in range(slices)]


def turned(pair, columns):
    if columns == 0:
        return pair
    moved = [pltpu.roll(p, columns % LANES, 1) for p in pair]
    lane = lax.broadcasted_iota(jnp.int32, pair[0].shape, 1)
    if columns > 0:
        return [moved[0], jnp.where(lane < columns, moved[0], moved[1])]
    return [jnp.where(lane >= LANES + columns, moved[1], moved[0]), moved[1]]


def encode(value, live):
    code = (value * lax.rsqrt(value) + 0.5).astype(jnp.int32)
    return jnp.where(live, code, -1)


def boundary(halo, own, keep, marks, pairs, slices):
    lane = lax.broadcasted_iota(jnp.int32, (EDGES, LANES), 1)
    slot = lax.rem(lane, 8)
    slab = lax.rem(lax.div(lane, 8), 8)
    raw = []
    for f in range(4):
        raw.append(jnp.where(slot < 3, halo[f].astype(jnp.float32), own[f].astype(jnp.float32)))
    color, through = classify(raw, marks, pairs)
    through = jnp.where((slot < 3) & (keep == 0), 1.0, through)
    alpha = 1.0 - through
    samples = [alpha * c for c in color] + [through]
    whole = lax.div(3 * slab, 8)
    frac = lax.rem(3 * slab, 8).astype(jnp.float32) * 0.125
    sheared = [jnp.zeros((EDGES, LANES), jnp.float32)] * 4
    for s in range(steps(slices)[-1][0] + 2):
        weight = jnp.where(whole == s, 1.0 - frac, 0.0) + jnp.where(whole + 1 == s, frac, 0.0)
        for c in range(4):
            moved = samples[c] if s == 0 else pltpu.roll(samples[c], s, 1)
            sheared[c] = sheared[c] + weight * moved
    product = sheared[3]
    for s in (1, 2, 4):
        product = product * jnp.where(slab >= s, pltpu.roll(product, 8 * s, 1), 1.0)
    before = jnp.where(slab >= 1, pltpu.roll(product, 8, 1), 1.0)
    result = []
    for c in range(3):
        total = before * sheared[c]
        for s in (1, 2, 4):
            total = total + jnp.where(slab >= s, pltpu.roll(total, 8 * s, 1), 0.0)
        result.append(total)
    return result + [CODE * CODE - CODE * CODE * product]


def edge_kernel(slices, bp_ref, color_ref, opacity_ref, live_ref, halo_ref, own_ref, codes_ref, out_ref, edge_ref):
    marks, pairs = tables(bp_ref, color_ref, opacity_ref)
    has_left = lax.axis_index("bx")
    lane = lax.broadcasted_iota(jnp.int32, (EDGES, LANES), 1)
    line = lax.broadcasted_iota(jnp.int32, (EDGES, LANES), 0)
    line = line + lax.div(line, SUB) * SUB + jnp.where(lane < 64, 0, SUB)
    for part in range(halo_ref.shape[1] // EDGES):
        rows = slice(part * EDGES, (part + 1) * EDGES)
        live = (line + 2 * EDGES * part >= live_ref[0]) & (line + 2 * EDGES * part < live_ref[1])
        halo, own = halo_ref[:, rows, :], own_ref[:, rows, :]
        for c, value in enumerate(boundary(halo, own, has_left, marks, pairs, slices)):
            edge_ref[c, rows, :] = encode(value, live)
    lane = lax.broadcasted_iota(jnp.int32, (4 * TILE, LANES), 1)
    count = SUB // TILE

    def patch(j, carry):
        for g in range(2):
            turn = (2 * LANES - (64 * g + 8 * (slices - 1) + 3)) % LANES
            for t in range(count):
                tile = (2 * j + g) * count + t
                at = pl.ds(pl.multiple_of((j * count + t) * TILE, TILE), TILE)
                edge = jnp.concatenate([edge_ref[c, at, :] for c in range(4)], axis=0)
                codes = jnp.where(lane < 3, pltpu.roll(edge, turn, 1), codes_ref[tile, :, :LANES].astype(jnp.int32))
                out_ref[tile, :, :LANES] = codes.astype(jnp.int16)
                out_ref[tile, :, LANES:] = codes_ref[tile, :, LANES:]
        return carry

    lax.fori_loop(0, codes_ref.shape[0] // (2 * count), patch, 0, unroll=PATCH)


def with_edges(slices, breakpoints, tf_color, tf_opacity, live, halo, own, codes):
    smem = pl.BlockSpec(memory_space=pltpu.SMEM)
    vmem = pl.BlockSpec(memory_space=pltpu.VMEM)
    return pl.pallas_call(
        functools.partial(edge_kernel, slices),
        in_specs=[smem, smem, smem, smem, vmem, vmem, vmem],
        out_specs=vmem,
        out_shape=jax.ShapeDtypeStruct(codes.shape, codes.dtype),
        scratch_shapes=[pltpu.VMEM((4, halo.shape[1], LANES), jnp.int32)],
        compiler_params=pltpu.CompilerParams(vmem_limit_bytes=40 * 1024 * 1024),
        name="edges",
    )(breakpoints, tf_color, tf_opacity, live, halo, own, codes)


def brick_kernel(slices, bp_ref, color_ref, opacity_ref, live_ref, fields_ref, out_ref, rim_ref, packed_ref):
    marks, pairs = tables(bp_ref, color_ref, opacity_ref)
    plan = steps(slices)
    first = pl.program_id(0) * BLOCK
    rows = GROUP
    wide = lax.broadcasted_iota(jnp.int32, (SUB, LANES), 1)
    own_columns = LANES - 3 * lax.axis_index("bz")

    def group(j, carry):
        base = pl.multiple_of(j * rows, rows)
        spot = pl.ds(pl.multiple_of(j * SUB, SUB), SUB)
        sums = {}

        def add(s, weight, color):
            for c in range(3):
                terms = [w * q[c] for w, q in zip(weight, color)]
                sums[s, c] = [p + q for p, q in zip(sums[s, c], terms)] if (s, c) in sums else terms

        through = None
        for k in range(slices):
            whole, frac = plan[k]
            color, clear, raws = [], [], []
            for side in range(2):
                raw = [
                    fields_ref[f, k, pl.ds(base, rows), side * LANES : (side + 1) * LANES].astype(jnp.float32) for f in range(4)
                ]
                raws.append(raw)
                some, clean = classify(raw, marks, pairs)
                color.append(some)
                clear.append(clean)
            for f in range(4):
                for g in range(2):
                    part = slice(SUB * g, SUB * g + SUB)
                    both = jnp.where(wide < 64, raws[0][f][part], raws[1][f][part])
                    begin = 64 * g + 8 * k
                    both = pltpu.roll(both, (begin + 3) % LANES, 1)
                    pltpu.store(packed_ref.at[f, spot], both, mask=(wide >= begin) & (wide < begin + 8))
            alpha = [1.0 - c for c in clear]
            if through is None:
                add(0, alpha, color)
                through = clear
                continue
            near = [t * (1.0 - frac) for t in through] if frac else through
            add(whole, [w * a for w, a in zip(turned(near, -whole), alpha)], color)
            after = [n * c for n, c in zip(near, turned(clear, whole))]
            if frac:
                far = [t * frac for t in through]
                add(whole + 1, [w * a for w, a in zip(turned(far, -whole - 1), alpha)], color)
                after = [p + n * c for p, n, c in zip(after, far, turned(clear, whole + 1))]
            through = after
        reach = plan[-1][0] + 2
        done = []
        for c in range(3):
            moved = [turned(sums[s, c], s) for s in range(reach)]
            done.append([sum(m[side] for m in moved) for side in range(2)])
        done.append([CODE * CODE - CODE * CODE * t for t in through])
        lane = lax.broadcasted_iota(jnp.int32, (TILE, LANES), 1)
        for r in range(rows // TILE):
            tile = (rows // TILE) * j + r
            row = lax.broadcasted_iota(jnp.int32, (TILE, LANES), 0) + (first + tile * TILE)
            live = [(row >= live_ref[0]) & (row < live_ref[1])]
            live.append(live[0] | (lane >= own_columns))
            for side in range(2):
                codes = [encode(done[c][side][r * TILE : (r + 1) * TILE], live[side]) for c in range(4)]
                out_ref[tile, :, side * LANES : (side + 1) * LANES] = jnp.concatenate(codes, axis=0).astype(jnp.int16)
        return carry

    lax.fori_loop(0, BLOCK // rows, group, 0, unroll=UNROLL)
    rim_ref[...] = packed_ref[...].astype(rim_ref.dtype)


def brick(breakpoints, tf_color, tf_opacity, live, fields):
    _, slices, height, width = fields.shape
    smem = pl.BlockSpec(memory_space=pltpu.SMEM)
    return pl.pallas_call(
        functools.partial(brick_kernel, slices),
        grid=(height // BLOCK,),
        in_specs=[smem, smem, smem, smem, pl.BlockSpec((4, slices, BLOCK, width), lambda i: (0, 0, i, 0))],
        out_specs=[
            pl.BlockSpec((BLOCK // TILE, 4 * TILE, width), lambda i: (i, 0, 0)),
            pl.BlockSpec((4, HALF, LANES), lambda i: (0, i, 0)),
        ],
        out_shape=[
            jax.ShapeDtypeStruct((height // TILE, 4 * TILE, width), jnp.int16),
            jax.ShapeDtypeStruct((4, height // 2, LANES), jnp.bfloat16),
        ],
        scratch_shapes=[pltpu.VMEM((4, HALF, LANES), jnp.float32)],
        compiler_params=pltpu.CompilerParams(vmem_limit_bytes=40 * 1024 * 1024),
        cost_estimate=pl.CostEstimate(flops=60 * slices * height * width, bytes_accessed=8 * slices * height * width, transcendentals=0),
        name="brick",
    )(breakpoints, tf_color, tf_opacity, live, fields)


def image_kernel(count_x, count_z, order_ref, codes_ref, out_ref):
    lane = lax.broadcasted_iota(jnp.int32, (4 * TILE, LANES), 1)

    def column(i, carry):
        def layer(k, state):
            image, through = list(state[:2]), list(state[2:])
            d = order_ref[i, k]
            moved = 3 * d
            own = i * count_z + d
            behind = jnp.maximum(i - 1, 0) * count_z + d
            left = codes_ref[own, :, :LANES].astype(jnp.int32)
            right = codes_ref[own, :, LANES:].astype(jnp.int32)
            before = codes_ref[behind, :, LANES:].astype(jnp.int32)
            before = jnp.where((left[:, :1] < 0) | (i == 0), 0, before)
            tail = lane >= LANES - moved
            for side, piece in enumerate((jnp.where(tail, before, left), jnp.where(tail, left, right))):
                root = jnp.maximum(pltpu.roll(piece, moved, 1), 0).astype(jnp.float32) * (1.0 / CODE)
                piece = root * root
                t = through[side]
                image[side] = image[side] + jnp.concatenate([t, t, t], axis=0) * piece[: 3 * TILE]
                through[side] = t - t * piece[3 * TILE :]
            return (*image, *through)

        none = jnp.zeros((3 * TILE, LANES), jnp.float32)
        clear = jnp.ones((TILE, LANES), jnp.float32)
        state = lax.fori_loop(0, count_z, layer, (none, none, clear, clear), unroll=DEPTHS)
        image, through = state[:2], state[2:]
        for side in range(2):
            at = pl.multiple_of((2 * i + side) * LANES, LANES)
            for c in range(3):
                out_ref[c, :, pl.ds(at, LANES)] = image[side][c * TILE : (c + 1) * TILE]
            out_ref[3, :, pl.ds(at, LANES)] = 1.0 - through[side]
        return carry

    lax.fori_loop(0, count_x, column, 0, unroll=COLUMNS)


def compose(order, codes, count_x, count_z):
    vmem = pl.BlockSpec(memory_space=pltpu.VMEM)
    return pl.pallas_call(
        functools.partial(image_kernel, count_x, count_z),
        in_specs=[pl.BlockSpec(memory_space=pltpu.SMEM), vmem],
        out_specs=vmem,
        out_shape=jax.ShapeDtypeStruct((4, TILE, count_x * 2 * LANES), jnp.float32),
        compiler_params=pltpu.CompilerParams(vmem_limit_bytes=40 * 1024 * 1024),
        name="compose",
    )(order, codes)


def per_device(fields, breakpoints, tf_color, tf_opacity, depth_order, live_rows):
    count_x, count_z = lax.axis_size("bx"), lax.axis_size("bz")
    live = live_rows.reshape(2)
    tf = (breakpoints, tf_color, tf_opacity, live)
    codes, rim = brick(*tf, fields)
    behind = lax.ppermute(rim, "bx", [(i, i + 1) for i in range(count_x - 1)])
    codes = with_edges(fields.shape[1], *tf, behind, rim, codes)
    codes = lax.all_to_all(codes, ("bx", "bz"), split_axis=0, concat_axis=0, tiled=True)
    return compose(depth_order, codes, count_x, count_z)


def solution(mesh):
    return jax.shard_map(
        per_device,
        mesh=mesh,
        in_specs=(P(None, "bz", None, "bx"), P(), P(), P(), P(), P("bx", "bz", None)),
        out_specs=P(None, ("bx", "bz"), None),
        check_vma=False,
    )
```

```python
import functools

import jax
import jax.numpy as jnp
from jax import lax
from jax.experimental import pallas as pl
from jax.experimental.pallas import tpu as pltpu
from jax.sharding import PartitionSpec as P

NBP = 8
LANES = 128
TILE = 8
BLOCK = 128
HALF = BLOCK // 2
GROUP = 16
SUB = GROUP // 2
UNROLL = 2
EDGES = 512
COLUMNS = 1
PATCH = 4
RIMS = 256
COPIES = 8
DEPTHS = 8
CODE = 32767.0
LOG2E = 1.4426950408889634


def tables(bp_ref, color_ref, opacity_ref):
    marks = [bp_ref[j].astype(jnp.float32) * (1.0 / 127.5) - 1.0 for j in range(NBP)]
    values = [[color_ref[j, c] for j in range(NBP)] for c in range(3)]
    values.append([opacity_ref[j] for j in range(NBP)])
    row = lax.broadcasted_iota(jnp.int32, (TILE, LANES), 0)

    def by_segment(scalars):
        table = jnp.full((TILE, LANES), scalars[0], jnp.float32)
        for j in range(1, NBP - 1):
            table = jnp.where(row >= j, scalars[j], table)
        return table

    low = by_segment(marks[: NBP - 1])
    width = by_segment(marks[1:]) - low
    pairs = []
    for c, value in enumerate(values):
        if c < 3:
            value = [v * (CODE * CODE) for v in value]
        start = by_segment(value[: NBP - 1])
        slope = (by_segment(value[1:]) - start) / width
        offset = start - slope * low
        if c == 3:
            slope, offset = -LOG2E * slope, -LOG2E * offset
        pairs.append((offset, slope))
    return marks, (by_segment(marks[1 : NBP - 1] + [2.0]), pairs)


def looked_up(table, index):
    return jnp.take_along_axis(table, index, axis=0, mode="promise_in_bounds")


def classify(raw, marks, pairs):
    h = jnp.tanh(raw[0] * 0.5)
    swirl = raw[1] * raw[1] + raw[2] * raw[2] + (raw[3] * raw[3] + 0.25)
    index = jnp.zeros(h.shape, jnp.int32)
    for j in range(2, NBP - 1, 2):
        index = jnp.where(h >= marks[j], j, index)
    between, pairs = pairs
    parts = []
    for r in range(0, h.shape[0], TILE):
        segment, level = index[r : r + TILE], h[r : r + TILE]
        segment = jnp.where(level >= looked_up(between, segment), segment + 1, segment)
        parts.append([looked_up(offset, segment) + looked_up(slope, segment) * level for offset, slope in pairs])
    looked = [p[0] if len(p) == 1 else jnp.concatenate(p, axis=0) for p in zip(*parts)]
    return looked[:3], jnp.exp2(looked[3] * swirl)


def steps(slices):
    return [(3 * k // 8, (3 * k % 8) / 8.0) for k in range(slices)]


def turned(pair, columns):
    if columns == 0:
        return pair
    moved = [pltpu.roll(p, columns % LANES, 1) for p in pair]
    lane = lax.broadcasted_iota(jnp.int32, pair[0].shape, 1)
    if columns > 0:
        return [moved[0], jnp.where(lane < columns, moved[0], moved[1])]
    return [jnp.where(lane >= LANES + columns, moved[1], moved[0]), moved[1]]


def encode(value, live):
    code = (value * lax.rsqrt(value) + 0.5).astype(jnp.int32)
    return jnp.where(live, code, -1)


def boundary(halo, own, keep, marks, pairs, slices):
    lane = lax.broadcasted_iota(jnp.int32, (EDGES, LANES), 1)
    slot = lax.rem(lane, 8)
    slab = lax.rem(lax.div(lane, 8), 8)
    raw = []
    for f in range(4):
        raw.append(jnp.where(slot < 3, halo[f].astype(jnp.float32), own[f].astype(jnp.float32)))
    color, through = classify(raw, marks, pairs)
    through = jnp.where((slot < 3) & (keep == 0), 1.0, through)
    alpha = 1.0 - through
    samples = [alpha * c for c in color] + [through]
    whole = lax.div(3 * slab, 8)
    frac = lax.rem(3 * slab, 8).astype(jnp.float32) * 0.125
    sheared = [jnp.zeros((EDGES, LANES), jnp.float32)] * 4
    for s in range(steps(slices)[-1][0] + 2):
        weight = jnp.where(whole == s, 1.0 - frac, 0.0) + jnp.where(whole + 1 == s, frac, 0.0)
        for c in range(4):
            moved = samples[c] if s == 0 else pltpu.roll(samples[c], s, 1)
            sheared[c] = sheared[c] + weight * moved
    product = sheared[3]
    for s in (1, 2, 4):
        product = product * jnp.where(slab >= s, pltpu.roll(product, 8 * s, 1), 1.0)
    before = jnp.where(slab >= 1, pltpu.roll(product, 8, 1), 1.0)
    result = []
    for c in range(3):
        total = before * sheared[c]
        for s in (1, 2, 4):
            total = total + jnp.where(slab >= s, pltpu.roll(total, 8 * s, 1), 0.0)
        result.append(total)
    return result + [CODE * CODE - CODE * CODE * product]


def edge_kernel(slices, bp_ref, color_ref, opacity_ref, live_ref, halo_ref, own_ref, codes_ref, out_ref, edge_ref, full_ref, sems):
    marks, pairs = tables(bp_ref, color_ref, opacity_ref)
    has_left = lax.axis_index("bx")
    lane = lax.broadcasted_iota(jnp.int32, (EDGES, LANES), 1)
    line = lax.broadcasted_iota(jnp.int32, (EDGES, LANES), 0)
    line = line + lax.div(line, SUB) * SUB + jnp.where(lane < 64, 0, SUB)
    for part in range(halo_ref.shape[1] // EDGES):
        rows = slice(part * EDGES, (part + 1) * EDGES)
        live = (line + 2 * EDGES * part >= live_ref[0]) & (line + 2 * EDGES * part < live_ref[1])
        halo, own = halo_ref[:, rows, :], own_ref[:, rows, :]
        for c, value in enumerate(boundary(halo, own, has_left, marks, pairs, slices)):
            edge_ref[c, rows, :] = encode(value, live)
    lane = lax.broadcasted_iota(jnp.int32, (4 * TILE, LANES), 1)
    count = SUB // TILE

    def patch(j, carry):
        for g in range(2):
            turn = (2 * LANES - (64 * g + 8 * (slices - 1) + 3)) % LANES
            for t in range(count):
                tile = (2 * j + g) * count + t
                at = pl.ds(pl.multiple_of((j * count + t) * TILE, TILE), TILE)
                edge = jnp.concatenate([edge_ref[c, at, :] for c in range(4)], axis=0)
                codes = jnp.where(lane < 3, pltpu.roll(edge, turn, 1), codes_ref[tile, :, :LANES].astype(jnp.int32))
                full_ref[tile, :, :LANES] = codes.astype(jnp.int16)
                full_ref[tile, :, LANES:] = codes_ref[tile, :, LANES:]
        return carry

    steps_each = codes_ref.shape[0] // (2 * count) // COPIES

    def move(part):
        tiles = pl.ds(part * (codes_ref.shape[0] // COPIES), codes_ref.shape[0] // COPIES)
        return pltpu.make_async_copy(full_ref.at[tiles], out_ref.at[tiles], sems.at[part])

    def leave(part, carry):
        lax.fori_loop(0, steps_each, lambda j, c: patch(part * steps_each + j, c), 0, unroll=PATCH)
        move(part).start()
        return carry

    lax.fori_loop(0, COPIES, leave, 0)
    for part in range(COPIES):
        move(part).wait()


def with_edges(slices, breakpoints, tf_color, tf_opacity, live, halo, own, codes):
    smem = pl.BlockSpec(memory_space=pltpu.SMEM)
    vmem = pl.BlockSpec(memory_space=pltpu.VMEM)
    return pl.pallas_call(
        functools.partial(edge_kernel, slices),
        in_specs=[smem, smem, smem, smem, vmem, vmem, vmem],
        out_specs=pl.BlockSpec(memory_space=pltpu.HBM),
        out_shape=pltpu.HBM(codes.shape, codes.dtype),
        scratch_shapes=[
            pltpu.VMEM((4, halo.shape[1], LANES), jnp.int32),
            pltpu.VMEM(codes.shape, codes.dtype),
            pltpu.SemaphoreType.DMA((COPIES,)),
        ],
        compiler_params=pltpu.CompilerParams(vmem_limit_bytes=40 * 1024 * 1024),
        name="edges",
    )(breakpoints, tf_color, tf_opacity, live, halo, own, codes)


def brick_kernel(slices, bp_ref, color_ref, opacity_ref, live_ref, fields_ref, out_ref):
    marks, pairs = tables(bp_ref, color_ref, opacity_ref)
    plan = steps(slices)
    first = pl.program_id(0) * BLOCK
    rows = GROUP
    own_columns = LANES - 3 * lax.axis_index("bz")

    def group(j, carry):
        base = pl.multiple_of(j * rows, rows)
        sums = {}

        def add(s, weight, color):
            for c in range(3):
                terms = [w * q[c] for w, q in zip(weight, color)]
                sums[s, c] = [p + q for p, q in zip(sums[s, c], terms)] if (s, c) in sums else terms

        through = None
        for k in range(slices):
            whole, frac = plan[k]
            color, clear = [], []
            for side in range(2):
                raw = [
                    fields_ref[f, k, pl.ds(base, rows), side * LANES : (side + 1) * LANES].astype(jnp.float32) for f in range(4)
                ]
                some, clean = classify(raw, marks, pairs)
                color.append(some)
                clear.append(clean)
            alpha = [1.0 - c for c in clear]
            if through is None:
                add(0, alpha, color)
                through = clear
                continue
            near = [t * (1.0 - frac) for t in through] if frac else through
            add(whole, [w * a for w, a in zip(turned(near, -whole), alpha)], color)
            after = [n * c for n, c in zip(near, turned(clear, whole))]
            if frac:
                far = [t * frac for t in through]
                add(whole + 1, [w * a for w, a in zip(turned(far, -whole - 1), alpha)], color)
                after = [p + n * c for p, n, c in zip(after, far, turned(clear, whole + 1))]
            through = after
        reach = plan[-1][0] + 2
        done = []
        for c in range(3):
            moved = [turned(sums[s, c], s) for s in range(reach)]
            done.append([sum(m[side] for m in moved) for side in range(2)])
        done.append([CODE * CODE - CODE * CODE * t for t in through])
        lane = lax.broadcasted_iota(jnp.int32, (TILE, LANES), 1)
        for r in range(rows // TILE):
            tile = (rows // TILE) * j + r
            row = lax.broadcasted_iota(jnp.int32, (TILE, LANES), 0) + (first + tile * TILE)
            live = [(row >= live_ref[0]) & (row < live_ref[1])]
            live.append(live[0] | (lane >= own_columns))
            for side in range(2):
                codes = [encode(done[c][side][r * TILE : (r + 1) * TILE], live[side]) for c in range(4)]
                out_ref[tile, :, side * LANES : (side + 1) * LANES] = jnp.concatenate(codes, axis=0).astype(jnp.int16)
        return carry

    lax.fori_loop(0, BLOCK // rows, group, 0, unroll=UNROLL)


def brick(breakpoints, tf_color, tf_opacity, live, fields):
    _, slices, height, width = fields.shape
    smem = pl.BlockSpec(memory_space=pltpu.SMEM)
    return pl.pallas_call(
        functools.partial(brick_kernel, slices),
        grid=(height // BLOCK,),
        in_specs=[smem, smem, smem, smem, pl.BlockSpec((4, slices, BLOCK, width), lambda i: (0, 0, i, 0))],
        out_specs=pl.BlockSpec((BLOCK // TILE, 4 * TILE, width), lambda i: (i, 0, 0)),
        out_shape=jax.ShapeDtypeStruct((height // TILE, 4 * TILE, width), jnp.int16),
        compiler_params=pltpu.CompilerParams(vmem_limit_bytes=40 * 1024 * 1024),
        cost_estimate=pl.CostEstimate(flops=60 * slices * height * width, bytes_accessed=8 * slices * height * width, transcendentals=0),
        name="brick",
    )(breakpoints, tf_color, tf_opacity, live, fields)


def rim_kernel(slices, fields_ref, rim_ref):
    rows = 4 * SUB
    lane = lax.broadcasted_iota(jnp.int32, (2 * SUB, LANES), 1)

    def group(j, carry):
        base = pl.multiple_of(j * rows, rows)
        for f in range(4):
            total = jnp.zeros((2 * SUB, LANES), jnp.float32)
            for k in range(slices):
                left = fields_ref[f, k, pl.ds(base, rows), :LANES].astype(jnp.float32)
                right = fields_ref[f, k, pl.ds(base, rows), LANES:].astype(jnp.float32)
                parts = [slice(SUB * p, SUB * (p + 1)) for p in range(4)]
                for g in range(2):
                    both = [jnp.where(lane[:SUB] < 64, left[p], right[p]) for p in parts[g::2]]
                    begin = 64 * g + 8 * k
                    both = pltpu.roll(jnp.concatenate(both, axis=0), (begin + 3) % LANES, 1)
                    total = jnp.where((lane >= begin) & (lane < begin + 8), both, total)
            rim_ref[f, pl.ds(pl.multiple_of(j * 2 * SUB, 2 * SUB), 2 * SUB), :] = total.astype(rim_ref.dtype)
        return carry

    lax.fori_loop(0, RIMS // rows, group, 0, unroll=2)


def rims(fields):
    _, slices, height, width = fields.shape
    return pl.pallas_call(
        functools.partial(rim_kernel, slices),
        grid=(height // RIMS,),
        in_specs=[pl.BlockSpec((4, slices, RIMS, width), lambda i: (0, 0, i, 0))],
        out_specs=pl.BlockSpec((4, RIMS // 2, LANES), lambda i: (0, i, 0)),
        out_shape=jax.ShapeDtypeStruct((4, height // 2, LANES), jnp.bfloat16),
        compiler_params=pltpu.CompilerParams(vmem_limit_bytes=40 * 1024 * 1024),
        cost_estimate=pl.CostEstimate(flops=4 * slices * height * width, bytes_accessed=8 * slices * height * width, transcendentals=0),
        name="rims",
    )(fields)


def image_kernel(count_x, count_z, order_ref, codes_ref, out_ref):
    lane = lax.broadcasted_iota(jnp.int32, (4 * TILE, LANES), 1)

    def column(i, carry):
        def layer(k, state):
            image, through = list(state[:2]), list(state[2:])
            d = order_ref[i, k]
            moved = 3 * d
            own = i * count_z + d
            behind = jnp.maximum(i - 1, 0) * count_z + d
            left = codes_ref[own, :, :LANES].astype(jnp.int32)
            right = codes_ref[own, :, LANES:].astype(jnp.int32)
            before = codes_ref[behind, :, LANES:].astype(jnp.int32)
            before = jnp.where(i == 0, 0, before)
            tail = lane >= LANES - moved
            for side, piece in enumerate((jnp.where(tail & (left >= 0), before, left), jnp.where(tail, left, right))):
                root = jnp.maximum(pltpu.roll(piece, moved, 1), 0).astype(jnp.float32) * (1.0 / CODE)
                piece = root * root
                t = through[side]
                image[side] = image[side] + jnp.concatenate([t, t, t], axis=0) * piece[: 3 * TILE]
                through[side] = t - t * piece[3 * TILE :]
            return (*image, *through)

        none = jnp.zeros((3 * TILE, LANES), jnp.float32)
        clear = jnp.ones((TILE, LANES), jnp.float32)
        state = lax.fori_loop(0, count_z, layer, (none, none, clear, clear), unroll=DEPTHS)
        image, through = state[:2], state[2:]
        for side in range(2):
            at = pl.multiple_of((2 * i + side) * LANES, LANES)
            for c in range(3):
                out_ref[c, :, pl.ds(at, LANES)] = image[side][c * TILE : (c + 1) * TILE]
            out_ref[3, :, pl.ds(at, LANES)] = 1.0 - through[side]
        return carry

    lax.fori_loop(0, count_x, column, 0, unroll=COLUMNS)


def compose(order, codes, count_x, count_z):
    vmem = pl.BlockSpec(memory_space=pltpu.VMEM)
    return pl.pallas_call(
        functools.partial(image_kernel, count_x, count_z),
        in_specs=[pl.BlockSpec(memory_space=pltpu.SMEM), vmem],
        out_specs=vmem,
        out_shape=jax.ShapeDtypeStruct((4, TILE, count_x * 2 * LANES), jnp.float32),
        compiler_params=pltpu.CompilerParams(vmem_limit_bytes=40 * 1024 * 1024),
        name="compose",
    )(order, codes)


def per_device(fields, breakpoints, tf_color, tf_opacity, depth_order, live_rows):
    count_x, count_z = lax.axis_size("bx"), lax.axis_size("bz")
    live = live_rows.reshape(2)
    tf = (breakpoints, tf_color, tf_opacity, live)
    rim = rims(fields)
    behind = lax.ppermute(rim, "bx", [(i, i + 1) for i in range(count_x - 1)])
    codes = with_edges(fields.shape[1], *tf, behind, rim, brick(*tf, fields))
    codes = lax.all_to_all(codes, ("bx", "bz"), split_axis=0, concat_axis=0, tiled=True)
    return compose(depth_order, codes, count_x, count_z)


def solution(mesh):
    return jax.shard_map(
        per_device,
        mesh=mesh,
        in_specs=(P(None, "bz", None, "bx"), P(), P(), P(), P(), P("bx", "bz", None)),
        out_specs=P(None, ("bx", "bz"), None),
        check_vma=False,
    )
```

```python
import functools

import jax
import jax.numpy as jnp
from jax import lax
from jax.experimental import pallas as pl
from jax.experimental.pallas import tpu as pltpu
from jax.sharding import PartitionSpec as P

NBP = 8
LANES = 128
TILE = 8
BLOCK = 128
HALF = BLOCK // 2
GROUP = 16
SUB = GROUP // 2
UNROLL = 2
EDGES = 512
COLUMNS = 2
PATCH = 8
RIMS = 256
COPIES = 4
DEPTHS = 8
CODE = 32767.0
LOG2E = 1.4426950408889634


def tables(bp_ref, color_ref, opacity_ref):
    marks = [bp_ref[j].astype(jnp.float32) * (1.0 / 127.5) - 1.0 for j in range(NBP)]
    values = [[color_ref[j, c] for j in range(NBP)] for c in range(3)]
    values.append([opacity_ref[j] for j in range(NBP)])
    row = lax.broadcasted_iota(jnp.int32, (TILE, LANES), 0)

    def by_segment(scalars):
        table = jnp.full((TILE, LANES), scalars[0], jnp.float32)
        for j in range(1, NBP - 1):
            table = jnp.where(row >= j, scalars[j], table)
        return table

    low = by_segment(marks[: NBP - 1])
    width = by_segment(marks[1:]) - low
    pairs = []
    for c, value in enumerate(values):
        if c < 3:
            value = [v * (CODE * CODE) for v in value]
        start = by_segment(value[: NBP - 1])
        slope = (by_segment(value[1:]) - start) / width
        offset = start - slope * low
        if c == 3:
            slope, offset = -LOG2E * slope, -LOG2E * offset
        pairs.append((offset, slope))
    return marks, (by_segment(marks[1 : NBP - 1] + [2.0]), pairs)


def looked_up(table, index):
    return jnp.take_along_axis(table, index, axis=0, mode="promise_in_bounds")


def classify(raw, marks, pairs):
    h = jnp.tanh(raw[0] * 0.5)
    swirl = raw[1] * raw[1] + raw[2] * raw[2] + (raw[3] * raw[3] + 0.25)
    index = jnp.zeros(h.shape, jnp.int32)
    for j in range(2, NBP - 1, 2):
        index = jnp.where(h >= marks[j], j, index)
    between, pairs = pairs
    parts = []
    for r in range(0, h.shape[0], TILE):
        segment, level = index[r : r + TILE], h[r : r + TILE]
        segment = jnp.where(level >= looked_up(between, segment), segment + 1, segment)
        parts.append([looked_up(offset, segment) + looked_up(slope, segment) * level for offset, slope in pairs])
    looked = [p[0] if len(p) == 1 else jnp.concatenate(p, axis=0) for p in zip(*parts)]
    return looked[:3], jnp.exp2(looked[3] * swirl)


def steps(slices):
    return [(3 * k // 8, (3 * k % 8) / 8.0) for k in range(slices)]


def turned(pair, columns):
    if columns == 0:
        return pair
    moved = [pltpu.roll(p, columns % LANES, 1) for p in pair]
    lane = lax.broadcasted_iota(jnp.int32, pair[0].shape, 1)
    if columns > 0:
        return [moved[0], jnp.where(lane < columns, moved[0], moved[1])]
    return [jnp.where(lane >= LANES + columns, moved[1], moved[0]), moved[1]]


def encode(value, live):
    code = (value * lax.rsqrt(value) + 0.5).astype(jnp.int32)
    return jnp.where(live, code, -1)


def boundary(halo, own, keep, marks, pairs, slices):
    lane = lax.broadcasted_iota(jnp.int32, (EDGES, LANES), 1)
    slot = lax.rem(lane, 8)
    slab = lax.rem(lax.div(lane, 8), 8)
    raw = []
    for f in range(4):
        raw.append(jnp.where(slot < 3, halo[f].astype(jnp.float32), own[f].astype(jnp.float32)))
    color, through = classify(raw, marks, pairs)
    through = jnp.where((slot < 3) & (keep == 0), 1.0, through)
    alpha = 1.0 - through
    samples = [alpha * c for c in color] + [through]
    whole = lax.div(3 * slab, 8)
    frac = lax.rem(3 * slab, 8).astype(jnp.float32) * 0.125
    sheared = [jnp.zeros((EDGES, LANES), jnp.float32)] * 4
    for s in range(steps(slices)[-1][0] + 2):
        weight = jnp.where(whole == s, 1.0 - frac, 0.0) + jnp.where(whole + 1 == s, frac, 0.0)
        for c in range(4):
            moved = samples[c] if s == 0 else pltpu.roll(samples[c], s, 1)
            sheared[c] = sheared[c] + weight * moved
    product = sheared[3]
    for s in (1, 2, 4):
        product = product * jnp.where(slab >= s, pltpu.roll(product, 8 * s, 1), 1.0)
    before = jnp.where(slab >= 1, pltpu.roll(product, 8, 1), 1.0)
    result = []
    for c in range(3):
        total = before * sheared[c]
        for s in (1, 2, 4):
            total = total + jnp.where(slab >= s, pltpu.roll(total, 8 * s, 1), 0.0)
        result.append(total)
    return result + [CODE * CODE - CODE * CODE * product]


def edge_kernel(slices, bp_ref, color_ref, opacity_ref, live_ref, halo_ref, own_ref, codes_ref, out_ref, edge_ref, full_ref, sems):
    marks, pairs = tables(bp_ref, color_ref, opacity_ref)
    has_left = lax.axis_index("bx")
    lane = lax.broadcasted_iota(jnp.int32, (EDGES, LANES), 1)
    line = lax.broadcasted_iota(jnp.int32, (EDGES, LANES), 0)
    line = line + lax.div(line, SUB) * SUB + jnp.where(lane < 64, 0, SUB)
    for part in range(halo_ref.shape[1] // EDGES):
        rows = slice(part * EDGES, (part + 1) * EDGES)
        live = (line + 2 * EDGES * part >= live_ref[0]) & (line + 2 * EDGES * part < live_ref[1])
        halo, own = halo_ref[:, rows, :], own_ref[:, rows, :]
        for c, value in enumerate(boundary(halo, own, has_left, marks, pairs, slices)):
            codes = encode(value, live)
            for g in range(2):
                edge_ref[g, c, rows, :] = pltpu.roll(codes, (2 * LANES - (64 * g + 8 * (slices - 1) + 3)) % LANES, 1)
    lane = lax.broadcasted_iota(jnp.int32, (4 * TILE, LANES), 1)
    count = SUB // TILE

    def patch(j, carry):
        for g in range(2):
            for t in range(count):
                tile = (2 * j + g) * count + t
                at = pl.ds(pl.multiple_of((j * count + t) * TILE, TILE), TILE)
                edge = jnp.concatenate([edge_ref[g, c, at, :] for c in range(4)], axis=0)
                codes = jnp.where(lane < 3, edge, codes_ref[tile, :, :LANES].astype(jnp.int32))
                full_ref[tile, :, :LANES] = codes.astype(jnp.int16)
                full_ref[tile, :, LANES:] = codes_ref[tile, :, LANES:]
        return carry

    steps_each = codes_ref.shape[0] // (2 * count) // COPIES

    def move(part):
        tiles = pl.ds(part * (codes_ref.shape[0] // COPIES), codes_ref.shape[0] // COPIES)
        return pltpu.make_async_copy(full_ref.at[tiles], out_ref.at[tiles], sems.at[part])

    def leave(part, carry):
        lax.fori_loop(0, steps_each, lambda j, c: patch(part * steps_each + j, c), 0, unroll=PATCH)
        move(part).start()
        return carry

    lax.fori_loop(0, COPIES, leave, 0)
    for part in range(COPIES):
        move(part).wait()


def with_edges(slices, breakpoints, tf_color, tf_opacity, live, halo, own, codes):
    smem = pl.BlockSpec(memory_space=pltpu.SMEM)
    vmem = pl.BlockSpec(memory_space=pltpu.VMEM)
    return pl.pallas_call(
        functools.partial(edge_kernel, slices),
        in_specs=[smem, smem, smem, smem, vmem, vmem, vmem],
        out_specs=pl.BlockSpec(memory_space=pltpu.HBM),
        out_shape=pltpu.HBM(codes.shape, codes.dtype),
        scratch_shapes=[
            pltpu.VMEM((2, 4, halo.shape[1], LANES), jnp.int32),
            pltpu.VMEM(codes.shape, codes.dtype),
            pltpu.SemaphoreType.DMA((COPIES,)),
        ],
        compiler_params=pltpu.CompilerParams(vmem_limit_bytes=40 * 1024 * 1024),
        name="edges",
    )(breakpoints, tf_color, tf_opacity, live, halo, own, codes)


def brick_kernel(slices, bp_ref, color_ref, opacity_ref, live_ref, fields_ref, out_ref):
    marks, pairs = tables(bp_ref, color_ref, opacity_ref)
    plan = steps(slices)
    first = pl.program_id(0) * BLOCK
    rows = GROUP
    own_columns = LANES - 3 * lax.axis_index("bz")

    def group(j, carry):
        base = pl.multiple_of(j * rows, rows)
        sums = {}

        def add(s, weight, color):
            for c in range(3):
                terms = [w * q[c] for w, q in zip(weight, color)]
                sums[s, c] = [p + q for p, q in zip(sums[s, c], terms)] if (s, c) in sums else terms

        through = None
        for k in range(slices):
            whole, frac = plan[k]
            color, clear = [], []
            for side in range(2):
                raw = [
                    fields_ref[f, k, pl.ds(base, rows), side * LANES : (side + 1) * LANES].astype(jnp.float32) for f in range(4)
                ]
                some, clean = classify(raw, marks, pairs)
                color.append(some)
                clear.append(clean)
            alpha = [1.0 - c for c in clear]
            if through is None:
                add(0, alpha, color)
                through = clear
                continue
            near = [t * (1.0 - frac) for t in through] if frac else through
            add(whole, [w * a for w, a in zip(turned(near, -whole), alpha)], color)
            after = [n * c for n, c in zip(near, turned(clear, whole))]
            if frac:
                far = [t * frac for t in through]
                add(whole + 1, [w * a for w, a in zip(turned(far, -whole - 1), alpha)], color)
                after = [p + n * c for p, n, c in zip(after, far, turned(clear, whole + 1))]
            through = after
        reach = plan[-1][0] + 2
        done = []
        for c in range(3):
            moved = [turned(sums[s, c], s) for s in range(reach)]
            done.append([sum(m[side] for m in moved) for side in range(2)])
        done.append([CODE * CODE - CODE * CODE * t for t in through])
        lane = lax.broadcasted_iota(jnp.int32, (TILE, LANES), 1)
        for r in range(rows // TILE):
            tile = (rows // TILE) * j + r
            row = lax.broadcasted_iota(jnp.int32, (TILE, LANES), 0) + (first + tile * TILE)
            live = [(row >= live_ref[0]) & (row < live_ref[1])]
            live.append(live[0] | (lane >= own_columns))
            for side in range(2):
                codes = [encode(done[c][side][r * TILE : (r + 1) * TILE], live[side]) for c in range(4)]
                out_ref[tile, :, side * LANES : (side + 1) * LANES] = jnp.concatenate(codes, axis=0).astype(jnp.int16)
        return carry

    lax.fori_loop(0, BLOCK // rows, group, 0, unroll=UNROLL)


def brick(breakpoints, tf_color, tf_opacity, live, fields):
    _, slices, height, width = fields.shape
    smem = pl.BlockSpec(memory_space=pltpu.SMEM)
    return pl.pallas_call(
        functools.partial(brick_kernel, slices),
        grid=(height // BLOCK,),
        in_specs=[smem, smem, smem, smem, pl.BlockSpec((4, slices, BLOCK, width), lambda i: (0, 0, i, 0))],
        out_specs=pl.BlockSpec((BLOCK // TILE, 4 * TILE, width), lambda i: (i, 0, 0)),
        out_shape=jax.ShapeDtypeStruct((height // TILE, 4 * TILE, width), jnp.int16),
        compiler_params=pltpu.CompilerParams(vmem_limit_bytes=40 * 1024 * 1024),
        cost_estimate=pl.CostEstimate(flops=60 * slices * height * width, bytes_accessed=8 * slices * height * width, transcendentals=0),
        name="brick",
    )(breakpoints, tf_color, tf_opacity, live, fields)


def rim_kernel(slices, fields_ref, rim_ref):
    rows = 4 * SUB
    lane = lax.broadcasted_iota(jnp.int32, (2 * SUB, LANES), 1)

    def group(j, carry):
        base = pl.multiple_of(j * rows, rows)
        for f in range(4):
            total = jnp.zeros((2 * SUB, LANES), jnp.float32)
            for k in range(slices):
                left = fields_ref[f, k, pl.ds(base, rows), :LANES].astype(jnp.float32)
                right = fields_ref[f, k, pl.ds(base, rows), LANES:].astype(jnp.float32)
                parts = [slice(SUB * p, SUB * (p + 1)) for p in range(4)]
                for g in range(2):
                    both = [jnp.where(lane[:SUB] < 64, left[p], right[p]) for p in parts[g::2]]
                    begin = 64 * g + 8 * k
                    both = pltpu.roll(jnp.concatenate(both, axis=0), (begin + 3) % LANES, 1)
                    total = jnp.where((lane >= begin) & (lane < begin + 8), both, total)
            rim_ref[f, pl.ds(pl.multiple_of(j * 2 * SUB, 2 * SUB), 2 * SUB), :] = total.astype(rim_ref.dtype)
        return carry

    lax.fori_loop(0, RIMS // rows, group, 0, unroll=2)


def rims(fields):
    _, slices, height, width = fields.shape
    return pl.pallas_call(
        functools.partial(rim_kernel, slices),
        grid=(height // RIMS,),
        in_specs=[pl.BlockSpec((4, slices, RIMS, width), lambda i: (0, 0, i, 0))],
        out_specs=pl.BlockSpec((4, RIMS // 2, LANES), lambda i: (0, i, 0)),
        out_shape=jax.ShapeDtypeStruct((4, height // 2, LANES), jnp.bfloat16),
        compiler_params=pltpu.CompilerParams(vmem_limit_bytes=40 * 1024 * 1024),
        cost_estimate=pl.CostEstimate(flops=4 * slices * height * width, bytes_accessed=8 * slices * height * width, transcendentals=0),
        name="rims",
    )(fields)


def image_kernel(count_x, count_z, order_ref, codes_ref, out_ref):
    lane = lax.broadcasted_iota(jnp.int32, (4 * TILE, LANES), 1)

    def column(i, carry):
        def layer(k, state):
            image, through = list(state[:2]), list(state[2:])
            d = order_ref[i, k]
            moved = 3 * d
            own = i * count_z + d
            behind = jnp.maximum(i - 1, 0) * count_z + d
            left = codes_ref[own, :, :LANES].astype(jnp.int32)
            right = codes_ref[own, :, LANES:].astype(jnp.int32)
            before = codes_ref[behind, :, LANES:].astype(jnp.int32)
            before = jnp.where(i == 0, 0, before)
            tail = lane >= LANES - moved
            for side, piece in enumerate((jnp.where(tail & (left >= 0), before, left), jnp.where(tail, left, right))):
                root = jnp.maximum(pltpu.roll(piece, moved, 1), 0).astype(jnp.float32) * (1.0 / CODE)
                piece = root * root
                t = through[side]
                image[side] = image[side] + jnp.concatenate([t, t, t], axis=0) * piece[: 3 * TILE]
                through[side] = t - t * piece[3 * TILE :]
            return (*image, *through)

        none = jnp.zeros((3 * TILE, LANES), jnp.float32)
        clear = jnp.ones((TILE, LANES), jnp.float32)
        state = lax.fori_loop(0, count_z, layer, (none, none, clear, clear), unroll=DEPTHS)
        image, through = state[:2], state[2:]
        for side in range(2):
            at = pl.multiple_of((2 * i + side) * LANES, LANES)
            for c in range(3):
                out_ref[c, :, pl.ds(at, LANES)] = image[side][c * TILE : (c + 1) * TILE]
            out_ref[3, :, pl.ds(at, LANES)] = 1.0 - through[side]
        return carry

    lax.fori_loop(0, count_x, column, 0, unroll=COLUMNS)


def compose(order, codes, count_x, count_z):
    vmem = pl.BlockSpec(memory_space=pltpu.VMEM)
    return pl.pallas_call(
        functools.partial(image_kernel, count_x, count_z),
        in_specs=[pl.BlockSpec(memory_space=pltpu.SMEM), vmem],
        out_specs=vmem,
        out_shape=jax.ShapeDtypeStruct((4, TILE, count_x * 2 * LANES), jnp.float32),
        compiler_params=pltpu.CompilerParams(vmem_limit_bytes=40 * 1024 * 1024),
        name="compose",
    )(order, codes)


def per_device(fields, breakpoints, tf_color, tf_opacity, depth_order, live_rows):
    count_x, count_z = lax.axis_size("bx"), lax.axis_size("bz")
    live = live_rows.reshape(2)
    tf = (breakpoints, tf_color, tf_opacity, live)
    rim = rims(fields)
    behind = lax.ppermute(rim, "bx", [(i, i + 1) for i in range(count_x - 1)])
    codes = with_edges(fields.shape[1], *tf, behind, rim, brick(*tf, fields))
    codes = lax.all_to_all(codes, ("bx", "bz"), split_axis=0, concat_axis=0, tiled=True)
    return compose(depth_order, codes, count_x, count_z)


def solution(mesh):
    return jax.shard_map(
        per_device,
        mesh=mesh,
        in_specs=(P(None, "bz", None, "bx"), P(), P(), P(), P(), P("bx", "bz", None)),
        out_specs=P(None, ("bx", "bz"), None),
        check_vma=False,
    )
```

```python
import functools

import jax
import jax.numpy as jnp
from jax import lax
from jax.experimental import pallas as pl
from jax.experimental.pallas import tpu as pltpu
from jax.sharding import PartitionSpec as P

NBP = 8
LANES = 128
TILE = 8
BLOCK = 128
HALF = BLOCK // 2
GROUP = 16
SUB = GROUP // 2
UNROLL = 2
EDGES = 512
COLUMNS = 2
PATCH = 8
RIMS = 256
COPIES = 4
DEPTHS = 8
CODE = 32767.0
LOG2E = 1.4426950408889634


def tables(bp_ref, color_ref, opacity_ref):
    marks = [bp_ref[j].astype(jnp.float32) * (1.0 / 127.5) - 1.0 for j in range(NBP)]
    values = [[color_ref[j, c] for j in range(NBP)] for c in range(3)]
    values.append([opacity_ref[j] for j in range(NBP)])
    row = lax.broadcasted_iota(jnp.int32, (TILE, LANES), 0)

    def by_segment(scalars):
        table = jnp.full((TILE, LANES), scalars[0], jnp.float32)
        for j in range(1, NBP - 1):
            table = jnp.where(row >= j, scalars[j], table)
        return table

    low = by_segment(marks[: NBP - 1])
    width = by_segment(marks[1:]) - low
    pairs = []
    for c, value in enumerate(values):
        if c < 3:
            value = [v * (CODE * CODE) for v in value]
        start = by_segment(value[: NBP - 1])
        slope = (by_segment(value[1:]) - start) / width
        offset = start - slope * low
        if c == 3:
            slope, offset = -LOG2E * slope, -LOG2E * offset
        pairs.append((offset, slope))
    return marks, pairs


def looked_up(table, index):
    return jnp.take_along_axis(table, index, axis=0, mode="promise_in_bounds")


def classify(raw, marks, pairs):
    h = jnp.tanh(raw[0] * 0.5)
    swirl = raw[1] * raw[1] + raw[2] * raw[2] + (raw[3] * raw[3] + 0.25)
    index = jnp.zeros(h.shape, jnp.int32)
    for j in range(1, NBP - 1):
        index = jnp.where(h >= marks[j], j, index)
    parts = []
    for r in range(0, h.shape[0], TILE):
        segment, level = index[r : r + TILE], h[r : r + TILE]
        parts.append([looked_up(offset, segment) + looked_up(slope, segment) * level for offset, slope in pairs])
    looked = [p[0] if len(p) == 1 else jnp.concatenate(p, axis=0) for p in zip(*parts)]
    return looked[:3], jnp.exp2(looked[3] * swirl)


def steps(slices):
    return [(3 * k // 8, (3 * k % 8) / 8.0) for k in range(slices)]


def turned(pair, columns):
    if columns == 0:
        return pair
    moved = [pltpu.roll(p, columns % LANES, 1) for p in pair]
    lane = lax.broadcasted_iota(jnp.int32, pair[0].shape, 1)
    if columns > 0:
        return [moved[0], jnp.where(lane < columns, moved[0], moved[1])]
    return [jnp.where(lane >= LANES + columns, moved[1], moved[0]), moved[1]]


def encode(value, live):
    code = (value * lax.rsqrt(value) + 0.5).astype(jnp.int32)
    return jnp.where(live, code, -1)


def boundary(halo, own, keep, marks, pairs, slices):
    lane = lax.broadcasted_iota(jnp.int32, (EDGES, LANES), 1)
    slot = lax.rem(lane, 8)
    slab = lax.rem(lax.div(lane, 8), 8)
    raw = []
    for f in range(4):
        raw.append(jnp.where(slot < 3, halo[f].astype(jnp.float32), own[f].astype(jnp.float32)))
    color, through = classify(raw, marks, pairs)
    through = jnp.where((slot < 3) & (keep == 0), 1.0, through)
    alpha = 1.0 - through
    samples = [alpha * c for c in color] + [through]
    whole = lax.div(3 * slab, 8)
    frac = lax.rem(3 * slab, 8).astype(jnp.float32) * 0.125
    sheared = [jnp.zeros((EDGES, LANES), jnp.float32)] * 4
    for s in range(steps(slices)[-1][0] + 2):
        weight = jnp.where(whole == s, 1.0 - frac, 0.0) + jnp.where(whole + 1 == s, frac, 0.0)
        for c in range(4):
            moved = samples[c] if s == 0 else pltpu.roll(samples[c], s, 1)
            sheared[c] = sheared[c] + weight * moved
    product = sheared[3]
    for s in (1, 2, 4):
        product = product * jnp.where(slab >= s, pltpu.roll(product, 8 * s, 1), 1.0)
    before = jnp.where(slab >= 1, pltpu.roll(product, 8, 1), 1.0)
    result = []
    for c in range(3):
        total = before * sheared[c]
        for s in (1, 2, 4):
            total = total + jnp.where(slab >= s, pltpu.roll(total, 8 * s, 1), 0.0)
        result.append(total)
    return result + [CODE * CODE - CODE * CODE * product]


def edge_kernel(slices, bp_ref, color_ref, opacity_ref, live_ref, halo_ref, own_ref, codes_ref, out_ref, edge_ref, full_ref, sems):
    marks, pairs = tables(bp_ref, color_ref, opacity_ref)
    has_left = lax.axis_index("bx")
    lane = lax.broadcasted_iota(jnp.int32, (EDGES, LANES), 1)
    line = lax.broadcasted_iota(jnp.int32, (EDGES, LANES), 0)
    line = line + lax.div(line, SUB) * SUB + jnp.where(lane < 64, 0, SUB)
    for part in range(halo_ref.shape[1] // EDGES):
        rows = slice(part * EDGES, (part + 1) * EDGES)
        live = (line + 2 * EDGES * part >= live_ref[0]) & (line + 2 * EDGES * part < live_ref[1])
        halo, own = halo_ref[:, rows, :], own_ref[:, rows, :]
        for c, value in enumerate(boundary(halo, own, has_left, marks, pairs, slices)):
            codes = encode(value, live)
            for g in range(2):
                edge_ref[g, c, rows, :] = pltpu.roll(codes, (2 * LANES - (64 * g + 8 * (slices - 1) + 3)) % LANES, 1)
    lane = lax.broadcasted_iota(jnp.int32, (4 * TILE, LANES), 1)
    count = SUB // TILE

    def patch(j, carry):
        for g in range(2):
            for t in range(count):
                tile = (2 * j + g) * count + t
                at = pl.ds(pl.multiple_of((j * count + t) * TILE, TILE), TILE)
                edge = jnp.concatenate([edge_ref[g, c, at, :] for c in range(4)], axis=0)
                codes = jnp.where(lane < 3, edge, codes_ref[tile, :, :LANES].astype(jnp.int32))
                full_ref[tile, :, :LANES] = codes.astype(jnp.int16)
                full_ref[tile, :, LANES:] = codes_ref[tile, :, LANES:]
        return carry

    steps_each = codes_ref.shape[0] // (2 * count) // COPIES

    def move(part):
        tiles = pl.ds(part * (codes_ref.shape[0] // COPIES), codes_ref.shape[0] // COPIES)
        return pltpu.make_async_copy(full_ref.at[tiles], out_ref.at[tiles], sems.at[part])

    def leave(part, carry):
        lax.fori_loop(0, steps_each, lambda j, c: patch(part * steps_each + j, c), 0, unroll=PATCH)
        move(part).start()
        return carry

    lax.fori_loop(0, COPIES, leave, 0)
    for part in range(COPIES):
        move(part).wait()


def with_edges(slices, breakpoints, tf_color, tf_opacity, live, halo, own, codes):
    smem = pl.BlockSpec(memory_space=pltpu.SMEM)
    vmem = pl.BlockSpec(memory_space=pltpu.VMEM)
    return pl.pallas_call(
        functools.partial(edge_kernel, slices),
        in_specs=[smem, smem, smem, smem, vmem, vmem, vmem],
        out_specs=pl.BlockSpec(memory_space=pltpu.HBM),
        out_shape=pltpu.HBM(codes.shape, codes.dtype),
        scratch_shapes=[
            pltpu.VMEM((2, 4, halo.shape[1], LANES), jnp.int32),
            pltpu.VMEM(codes.shape, codes.dtype),
            pltpu.SemaphoreType.DMA((COPIES,)),
        ],
        compiler_params=pltpu.CompilerParams(vmem_limit_bytes=40 * 1024 * 1024),
        name="edges",
    )(breakpoints, tf_color, tf_opacity, live, halo, own, codes)


def brick_kernel(slices, bp_ref, color_ref, opacity_ref, live_ref, fields_ref, out_ref):
    marks, pairs = tables(bp_ref, color_ref, opacity_ref)
    plan = steps(slices)
    first = pl.program_id(0) * BLOCK
    rows = GROUP
    own_columns = LANES - 3 * lax.axis_index("bz")

    def group(j, carry):
        base = pl.multiple_of(j * rows, rows)
        sums = {}

        def add(s, weight, color):
            for c in range(3):
                terms = [w * q[c] for w, q in zip(weight, color)]
                sums[s, c] = [p + q for p, q in zip(sums[s, c], terms)] if (s, c) in sums else terms

        through = None
        for k in range(slices):
            whole, frac = plan[k]
            color, clear = [], []
            for side in range(2):
                raw = [
                    fields_ref[f, k, pl.ds(base, rows), side * LANES : (side + 1) * LANES].astype(jnp.float32) for f in range(4)
                ]
                some, clean = classify(raw, marks, pairs)
                color.append(some)
                clear.append(clean)
            alpha = [1.0 - c for c in clear]
            if through is None:
                add(0, alpha, color)
                through = clear
                continue
            near = [t * (1.0 - frac) for t in through] if frac else through
            add(whole, [w * a for w, a in zip(turned(near, -whole), alpha)], color)
            after = [n * c for n, c in zip(near, turned(clear, whole))]
            if frac:
                far = [t * frac for t in through]
                add(whole + 1, [w * a for w, a in zip(turned(far, -whole - 1), alpha)], color)
                after = [p + n * c for p, n, c in zip(after, far, turned(clear, whole + 1))]
            through = after
        reach = plan[-1][0] + 2
        done = []
        for c in range(3):
            moved = [turned(sums[s, c], s) for s in range(reach)]
            done.append([sum(m[side] for m in moved) for side in range(2)])
        done.append([CODE * CODE - CODE * CODE * t for t in through])
        lane = lax.broadcasted_iota(jnp.int32, (TILE, LANES), 1)
        for r in range(rows // TILE):
            tile = (rows // TILE) * j + r
            row = lax.broadcasted_iota(jnp.int32, (TILE, LANES), 0) + (first + tile * TILE)
            live = [(row >= live_ref[0]) & (row < live_ref[1])]
            live.append(live[0] | (lane >= own_columns))
            for side in range(2):
                codes = [encode(done[c][side][r * TILE : (r + 1) * TILE], live[side]) for c in range(4)]
                out_ref[tile, :, side * LANES : (side + 1) * LANES] = jnp.concatenate(codes, axis=0).astype(jnp.int16)
        return carry

    lax.fori_loop(0, BLOCK // rows, group, 0, unroll=UNROLL)


def brick(breakpoints, tf_color, tf_opacity, live, fields):
    _, slices, height, width = fields.shape
    smem = pl.BlockSpec(memory_space=pltpu.SMEM)
    return pl.pallas_call(
        functools.partial(brick_kernel, slices),
        grid=(height // BLOCK,),
        in_specs=[smem, smem, smem, smem, pl.BlockSpec((4, slices, BLOCK, width), lambda i: (0, 0, i, 0))],
        out_specs=pl.BlockSpec((BLOCK // TILE, 4 * TILE, width), lambda i: (i, 0, 0)),
        out_shape=jax.ShapeDtypeStruct((height // TILE, 4 * TILE, width), jnp.int16),
        compiler_params=pltpu.CompilerParams(vmem_limit_bytes=40 * 1024 * 1024),
        cost_estimate=pl.CostEstimate(flops=60 * slices * height * width, bytes_accessed=8 * slices * height * width, transcendentals=0),
        name="brick",
    )(breakpoints, tf_color, tf_opacity, live, fields)


def rim_kernel(slices, fields_ref, rim_ref):
    rows = 4 * SUB
    lane = lax.broadcasted_iota(jnp.int32, (2 * SUB, LANES), 1)

    def group(j, carry):
        base = pl.multiple_of(j * rows, rows)
        for f in range(4):
            total = jnp.zeros((2 * SUB, LANES), jnp.float32)
            for k in range(slices):
                left = fields_ref[f, k, pl.ds(base, rows), :LANES].astype(jnp.float32)
                right = fields_ref[f, k, pl.ds(base, rows), LANES:].astype(jnp.float32)
                parts = [slice(SUB * p, SUB * (p + 1)) for p in range(4)]
                for g in range(2):
                    both = [jnp.where(lane[:SUB] < 64, left[p], right[p]) for p in parts[g::2]]
                    begin = 64 * g + 8 * k
                    both = pltpu.roll(jnp.concatenate(both, axis=0), (begin + 3) % LANES, 1)
                    total = jnp.where((lane >= begin) & (lane < begin + 8), both, total)
            rim_ref[f, pl.ds(pl.multiple_of(j * 2 * SUB, 2 * SUB), 2 * SUB), :] = total.astype(rim_ref.dtype)
        return carry

    lax.fori_loop(0, RIMS // rows, group, 0, unroll=2)


def rims(fields):
    _, slices, height, width = fields.shape
    return pl.pallas_call(
        functools.partial(rim_kernel, slices),
        grid=(height // RIMS,),
        in_specs=[pl.BlockSpec((4, slices, RIMS, width), lambda i: (0, 0, i, 0))],
        out_specs=pl.BlockSpec((4, RIMS // 2, LANES), lambda i: (0, i, 0)),
        out_shape=jax.ShapeDtypeStruct((4, height // 2, LANES), jnp.bfloat16),
        compiler_params=pltpu.CompilerParams(vmem_limit_bytes=40 * 1024 * 1024),
        cost_estimate=pl.CostEstimate(flops=4 * slices * height * width, bytes_accessed=8 * slices * height * width, transcendentals=0),
        name="rims",
    )(fields)


def image_kernel(count_x, count_z, order_ref, codes_ref, out_ref):
    lane = lax.broadcasted_iota(jnp.int32, (4 * TILE, LANES), 1)

    def column(i, carry):
        def layer(k, state):
            image, through = list(state[:2]), list(state[2:])
            d = order_ref[i, k]
            moved = 3 * d
            own = i * count_z + d
            behind = jnp.maximum(i - 1, 0) * count_z + d
            left = codes_ref[own, :, :LANES].astype(jnp.int32)
            right = codes_ref[own, :, LANES:].astype(jnp.int32)
            before = codes_ref[behind, :, LANES:].astype(jnp.int32)
            before = jnp.where(i == 0, 0, before)
            tail = lane >= LANES - moved
            for side, piece in enumerate((jnp.where(tail & (left >= 0), before, left), jnp.where(tail, left, right))):
                root = jnp.maximum(pltpu.roll(piece, moved, 1), 0).astype(jnp.float32) * (1.0 / CODE)
                piece = root * root
                t = through[side]
                image[side] = image[side] + jnp.concatenate([t, t, t], axis=0) * piece[: 3 * TILE]
                through[side] = t - t * piece[3 * TILE :]
            return (*image, *through)

        none = jnp.zeros((3 * TILE, LANES), jnp.float32)
        clear = jnp.ones((TILE, LANES), jnp.float32)
        state = lax.fori_loop(0, count_z, layer, (none, none, clear, clear), unroll=DEPTHS)
        image, through = state[:2], state[2:]
        for side in range(2):
            at = pl.multiple_of((2 * i + side) * LANES, LANES)
            for c in range(3):
                out_ref[c, :, pl.ds(at, LANES)] = image[side][c * TILE : (c + 1) * TILE]
            out_ref[3, :, pl.ds(at, LANES)] = 1.0 - through[side]
        return carry

    lax.fori_loop(0, count_x, column, 0, unroll=COLUMNS)


def compose(order, codes, count_x, count_z):
    vmem = pl.BlockSpec(memory_space=pltpu.VMEM)
    return pl.pallas_call(
        functools.partial(image_kernel, count_x, count_z),
        in_specs=[pl.BlockSpec(memory_space=pltpu.SMEM), vmem],
        out_specs=vmem,
        out_shape=jax.ShapeDtypeStruct((4, TILE, count_x * 2 * LANES), jnp.float32),
        compiler_params=pltpu.CompilerParams(vmem_limit_bytes=40 * 1024 * 1024),
        name="compose",
    )(order, codes)


def per_device(fields, breakpoints, tf_color, tf_opacity, depth_order, live_rows):
    count_x, count_z = lax.axis_size("bx"), lax.axis_size("bz")
    live = live_rows.reshape(2)
    tf = (breakpoints, tf_color, tf_opacity, live)
    rim = rims(fields)
    behind = lax.ppermute(rim, "bx", [(i, i + 1) for i in range(count_x - 1)])
    codes = with_edges(fields.shape[1], *tf, behind, rim, brick(*tf, fields))
    codes = lax.all_to_all(codes, ("bx", "bz"), split_axis=0, concat_axis=0, tiled=True)
    return compose(depth_order, codes, count_x, count_z)


def solution(mesh):
    return jax.shard_map(
        per_device,
        mesh=mesh,
        in_specs=(P(None, "bz", None, "bx"), P(), P(), P(), P(), P("bx", "bz", None)),
        out_specs=P(None, ("bx", "bz"), None),
        check_vma=False,
    )
```

```python
import functools

import jax
import jax.numpy as jnp
from jax import lax
from jax.experimental import pallas as pl
from jax.experimental.pallas import tpu as pltpu
from jax.sharding import PartitionSpec as P

NBP = 8
LANES = 128
TILE = 8
BLOCK = 128
HALF = BLOCK // 2
GROUP = 16
SUB = GROUP // 2
UNROLL = 2
EDGES = 512
COLUMNS = 2
PATCH = 8
RIMS = 256
COPIES = 4
DEPTHS = 8
CODE = 32767.0
LOG2E = 1.4426950408889634


def tables(bp_ref, color_ref, opacity_ref):
    marks = [bp_ref[j].astype(jnp.float32) * (1.0 / 127.5) - 1.0 for j in range(NBP)]
    values = [[color_ref[j, c] for j in range(NBP)] for c in range(3)]
    values.append([opacity_ref[j] for j in range(NBP)])
    row = lax.broadcasted_iota(jnp.int32, (TILE, LANES), 0)

    def by_segment(scalars):
        table = jnp.full((TILE, LANES), scalars[0], jnp.float32)
        for j in range(1, NBP - 1):
            table = jnp.where(row >= j, scalars[j], table)
        return table

    low = by_segment(marks[: NBP - 1])
    width = by_segment(marks[1:]) - low
    pairs = []
    for c, value in enumerate(values):
        if c < 3:
            value = [v * (CODE * CODE) for v in value]
        start = by_segment(value[: NBP - 1])
        slope = (by_segment(value[1:]) - start) / width
        offset = start - slope * low
        if c == 3:
            slope, offset = -LOG2E * slope, -LOG2E * offset
        pairs.append((offset, slope))
    return marks, pairs


def looked_up(table, index):
    return jnp.take_along_axis(table, index, axis=0, mode="promise_in_bounds")


def classify(raw, marks, pairs):
    h = jnp.tanh(raw[0] * 0.5)
    swirl = raw[1] * raw[1] + raw[2] * raw[2] + (raw[3] * raw[3] + 0.25)
    index = jnp.zeros(h.shape, jnp.int32)
    for j in range(1, NBP - 1):
        index = jnp.where(h >= marks[j], j, index)
    parts = []
    for r in range(0, h.shape[0], TILE):
        segment, level = index[r : r + TILE], h[r : r + TILE]
        parts.append([looked_up(offset, segment) + looked_up(slope, segment) * level for offset, slope in pairs])
    looked = [p[0] if len(p) == 1 else jnp.concatenate(p, axis=0) for p in zip(*parts)]
    return looked[:3], jnp.exp2(looked[3] * swirl)


def steps(slices):
    return [(3 * k // 8, (3 * k % 8) / 8.0) for k in range(slices)]


def turned(pair, columns):
    if columns == 0:
        return pair
    moved = [pltpu.roll(p, columns % LANES, 1) for p in pair]
    lane = lax.broadcasted_iota(jnp.int32, pair[0].shape, 1)
    if columns > 0:
        return [moved[0], jnp.where(lane < columns, moved[0], moved[1])]
    return [jnp.where(lane >= LANES + columns, moved[1], moved[0]), moved[1]]


def encode(value, live):
    code = (value * lax.rsqrt(value) + 0.5).astype(jnp.int32)
    return jnp.where(live, code, -1)


def boundary(halo, own, keep, marks, pairs, slices):
    lane = lax.broadcasted_iota(jnp.int32, (EDGES, LANES), 1)
    slot = lax.rem(lane, 8)
    slab = lax.rem(lax.div(lane, 8), 8)
    raw = []
    for f in range(4):
        raw.append(jnp.where(slot < 3, halo[f].astype(jnp.float32), own[f].astype(jnp.float32)))
    color, through = classify(raw, marks, pairs)
    through = jnp.where((slot < 3) & (keep == 0), 1.0, through)
    alpha = 1.0 - through
    samples = [alpha * c for c in color] + [through]
    whole = lax.div(3 * slab, 8)
    frac = lax.rem(3 * slab, 8).astype(jnp.float32) * 0.125
    sheared = [jnp.zeros((EDGES, LANES), jnp.float32)] * 4
    for s in range(steps(slices)[-1][0] + 2):
        weight = jnp.where(whole == s, 1.0 - frac, 0.0) + jnp.where(whole + 1 == s, frac, 0.0)
        for c in range(4):
            moved = samples[c] if s == 0 else pltpu.roll(samples[c], s, 1)
            sheared[c] = sheared[c] + weight * moved
    product = sheared[3]
    for s in (1, 2, 4):
        product = product * jnp.where(slab >= s, pltpu.roll(product, 8 * s, 1), 1.0)
    before = jnp.where(slab >= 1, pltpu.roll(product, 8, 1), 1.0)
    result = []
    for c in range(3):
        total = before * sheared[c]
        for s in (1, 2, 4):
            total = total + jnp.where(slab >= s, pltpu.roll(total, 8 * s, 1), 0.0)
        result.append(total)
    return result + [CODE * CODE - CODE * CODE * product]


def edge_kernel(slices, bp_ref, color_ref, opacity_ref, live_ref, halo_ref, own_ref, codes_ref, out_ref, edge_ref, full_ref, sems):
    right = pl.ds(LANES, LANES)
    whole = pltpu.make_async_copy(codes_ref.at[:, :, right], out_ref.at[:, :, right], sems.at[COPIES])
    whole.start()
    marks, pairs = tables(bp_ref, color_ref, opacity_ref)
    has_left = lax.axis_index("bx")
    lane = lax.broadcasted_iota(jnp.int32, (EDGES, LANES), 1)
    line = lax.broadcasted_iota(jnp.int32, (EDGES, LANES), 0)
    line = line + lax.div(line, SUB) * SUB + jnp.where(lane < 64, 0, SUB)
    for part in range(halo_ref.shape[1] // EDGES):
        rows = slice(part * EDGES, (part + 1) * EDGES)
        live = (line + 2 * EDGES * part >= live_ref[0]) & (line + 2 * EDGES * part < live_ref[1])
        halo, own = halo_ref[:, rows, :], own_ref[:, rows, :]
        for c, value in enumerate(boundary(halo, own, has_left, marks, pairs, slices)):
            codes = encode(value, live)
            for g in range(2):
                edge_ref[g, c, rows, :] = pltpu.roll(codes, (2 * LANES - (64 * g + 8 * (slices - 1) + 3)) % LANES, 1)
    lane = lax.broadcasted_iota(jnp.int32, (4 * TILE, LANES), 1)
    count = SUB // TILE

    def patch(j, carry):
        for g in range(2):
            for t in range(count):
                tile = (2 * j + g) * count + t
                at = pl.ds(pl.multiple_of((j * count + t) * TILE, TILE), TILE)
                edge = jnp.concatenate([edge_ref[g, c, at, :] for c in range(4)], axis=0)
                codes = jnp.where(lane < 3, edge, codes_ref[tile, :, :LANES].astype(jnp.int32))
                full_ref[tile] = codes.astype(jnp.int16)
        return carry

    steps_each = codes_ref.shape[0] // (2 * count) // COPIES

    def move(part):
        tiles = pl.ds(part * (codes_ref.shape[0] // COPIES), codes_ref.shape[0] // COPIES)
        return pltpu.make_async_copy(full_ref.at[tiles], out_ref.at[tiles, :, pl.ds(0, LANES)], sems.at[part])

    def leave(part, carry):
        lax.fori_loop(0, steps_each, lambda j, c: patch(part * steps_each + j, c), 0, unroll=PATCH)
        move(part).start()
        return carry

    lax.fori_loop(0, COPIES, leave, 0)
    for part in range(COPIES):
        move(part).wait()
    whole.wait()


def with_edges(slices, breakpoints, tf_color, tf_opacity, live, halo, own, codes):
    smem = pl.BlockSpec(memory_space=pltpu.SMEM)
    vmem = pl.BlockSpec(memory_space=pltpu.VMEM)
    return pl.pallas_call(
        functools.partial(edge_kernel, slices),
        in_specs=[smem, smem, smem, smem, vmem, vmem, vmem],
        out_specs=pl.BlockSpec(memory_space=pltpu.HBM),
        out_shape=pltpu.HBM(codes.shape, codes.dtype),
        scratch_shapes=[
            pltpu.VMEM((2, 4, halo.shape[1], LANES), jnp.int32),
            pltpu.VMEM((*codes.shape[:2], LANES), codes.dtype),
            pltpu.SemaphoreType.DMA((COPIES + 1,)),
        ],
        compiler_params=pltpu.CompilerParams(vmem_limit_bytes=40 * 1024 * 1024),
        name="edges",
    )(breakpoints, tf_color, tf_opacity, live, halo, own, codes)


def brick_kernel(slices, bp_ref, color_ref, opacity_ref, live_ref, fields_ref, out_ref):
    marks, pairs = tables(bp_ref, color_ref, opacity_ref)
    plan = steps(slices)
    first = pl.program_id(0) * BLOCK
    rows = GROUP
    own_columns = LANES - 3 * lax.axis_index("bz")

    def group(j, carry):
        base = pl.multiple_of(j * rows, rows)
        sums = {}

        def add(s, weight, color):
            for c in range(3):
                terms = [w * q[c] for w, q in zip(weight, color)]
                sums[s, c] = [p + q for p, q in zip(sums[s, c], terms)] if (s, c) in sums else terms

        through = None
        for k in range(slices):
            whole, frac = plan[k]
            color, clear = [], []
            for side in range(2):
                raw = [
                    fields_ref[f, k, pl.ds(base, rows), side * LANES : (side + 1) * LANES].astype(jnp.float32) for f in range(4)
                ]
                some, clean = classify(raw, marks, pairs)
                color.append(some)
                clear.append(clean)
            alpha = [1.0 - c for c in clear]
            if through is None:
                add(0, alpha, color)
                through = clear
                continue
            near = [t * (1.0 - frac) for t in through] if frac else through
            add(whole, [w * a for w, a in zip(turned(near, -whole), alpha)], color)
            after = [n * c for n, c in zip(near, turned(clear, whole))]
            if frac:
                far = [t * frac for t in through]
                add(whole + 1, [w * a for w, a in zip(turned(far, -whole - 1), alpha)], color)
                after = [p + n * c for p, n, c in zip(after, far, turned(clear, whole + 1))]
            through = after
        reach = plan[-1][0] + 2
        done = []
        for c in range(3):
            moved = [turned(sums[s, c], s) for s in range(reach)]
            done.append([functools.reduce(jnp.add, [m[side] for m in moved]) for side in range(2)])
        done.append([CODE * CODE - CODE * CODE * t for t in through])
        lane = lax.broadcasted_iota(jnp.int32, (TILE, LANES), 1)
        for r in range(rows // TILE):
            tile = (rows // TILE) * j + r
            row = lax.broadcasted_iota(jnp.int32, (TILE, LANES), 0) + (first + tile * TILE)
            live = [(row >= live_ref[0]) & (row < live_ref[1])]
            live.append(live[0] | (lane >= own_columns))
            for side in range(2):
                codes = [encode(done[c][side][r * TILE : (r + 1) * TILE], live[side]) for c in range(4)]
                out_ref[tile, :, side * LANES : (side + 1) * LANES] = jnp.concatenate(codes, axis=0).astype(jnp.int16)
        return carry

    lax.fori_loop(0, BLOCK // rows, group, 0, unroll=UNROLL)


def brick(breakpoints, tf_color, tf_opacity, live, fields):
    _, slices, height, width = fields.shape
    smem = pl.BlockSpec(memory_space=pltpu.SMEM)
    return pl.pallas_call(
        functools.partial(brick_kernel, slices),
        grid=(height // BLOCK,),
        in_specs=[smem, smem, smem, smem, pl.BlockSpec((4, slices, BLOCK, width), lambda i: (0, 0, i, 0))],
        out_specs=pl.BlockSpec((BLOCK // TILE, 4 * TILE, width), lambda i: (i, 0, 0)),
        out_shape=jax.ShapeDtypeStruct((height // TILE, 4 * TILE, width), jnp.int16),
        compiler_params=pltpu.CompilerParams(vmem_limit_bytes=40 * 1024 * 1024),
        cost_estimate=pl.CostEstimate(flops=60 * slices * height * width, bytes_accessed=8 * slices * height * width, transcendentals=0),
        name="brick",
    )(breakpoints, tf_color, tf_opacity, live, fields)


def rim_kernel(slices, fields_ref, rim_ref):
    rows = 4 * SUB
    lane = lax.broadcasted_iota(jnp.int32, (2 * SUB, LANES), 1)

    def group(j, carry):
        base = pl.multiple_of(j * rows, rows)
        for f in range(4):
            total = jnp.zeros((2 * SUB, LANES), jnp.float32)
            for k in range(slices):
                left = fields_ref[f, k, pl.ds(base, rows), :LANES].astype(jnp.float32)
                right = fields_ref[f, k, pl.ds(base, rows), LANES:].astype(jnp.float32)
                parts = [slice(SUB * p, SUB * (p + 1)) for p in range(4)]
                for g in range(2):
                    both = [jnp.where(lane[:SUB] < 64, left[p], right[p]) for p in parts[g::2]]
                    begin = 64 * g + 8 * k
                    both = pltpu.roll(jnp.concatenate(both, axis=0), (begin + 3) % LANES, 1)
                    total = jnp.where((lane >= begin) & (lane < begin + 8), both, total)
            rim_ref[f, pl.ds(pl.multiple_of(j * 2 * SUB, 2 * SUB), 2 * SUB), :] = total.astype(rim_ref.dtype)
        return carry

    lax.fori_loop(0, RIMS // rows, group, 0, unroll=2)


def rims(fields):
    _, slices, height, width = fields.shape
    return pl.pallas_call(
        functools.partial(rim_kernel, slices),
        grid=(height // RIMS,),
        in_specs=[pl.BlockSpec((4, slices, RIMS, width), lambda i: (0, 0, i, 0))],
        out_specs=pl.BlockSpec((4, RIMS // 2, LANES), lambda i: (0, i, 0)),
        out_shape=jax.ShapeDtypeStruct((4, height // 2, LANES), jnp.bfloat16),
        compiler_params=pltpu.CompilerParams(vmem_limit_bytes=40 * 1024 * 1024),
        cost_estimate=pl.CostEstimate(flops=4 * slices * height * width, bytes_accessed=8 * slices * height * width, transcendentals=0),
        name="rims",
    )(fields)


def image_kernel(count_x, count_z, order_ref, codes_ref, out_ref):
    lane = lax.broadcasted_iota(jnp.int32, (4 * TILE, LANES), 1)

    def column(i, carry):
        def layer(k, state):
            image, through = list(state[:2]), list(state[2:])
            d = order_ref[i, k]
            moved = 3 * d
            own = i * count_z + d
            behind = jnp.maximum(i - 1, 0) * count_z + d
            left = codes_ref[own, :, :LANES].astype(jnp.int32)
            right = codes_ref[own, :, LANES:].astype(jnp.int32)
            before = codes_ref[behind, :, LANES:].astype(jnp.int32)
            before = jnp.where(i == 0, 0, before)
            tail = lane >= LANES - moved
            for side, piece in enumerate((jnp.where(tail & (left >= 0), before, left), jnp.where(tail, left, right))):
                root = jnp.maximum(pltpu.roll(piece, moved, 1), 0).astype(jnp.float32) * (1.0 / CODE)
                piece = root * root
                t = through[side]
                image[side] = image[side] + jnp.concatenate([t, t, t], axis=0) * piece[: 3 * TILE]
                through[side] = t - t * piece[3 * TILE :]
            return (*image, *through)

        none = jnp.zeros((3 * TILE, LANES), jnp.float32)
        clear = jnp.ones((TILE, LANES), jnp.float32)
        state = lax.fori_loop(0, count_z, layer, (none, none, clear, clear), unroll=DEPTHS)
        image, through = state[:2], state[2:]
        for side in range(2):
            at = pl.multiple_of((2 * i + side) * LANES, LANES)
            for c in range(3):
                out_ref[c, :, pl.ds(at, LANES)] = image[side][c * TILE : (c + 1) * TILE]
            out_ref[3, :, pl.ds(at, LANES)] = 1.0 - through[side]
        return carry

    lax.fori_loop(0, count_x, column, 0, unroll=COLUMNS)


def compose(order, codes, count_x, count_z):
    vmem = pl.BlockSpec(memory_space=pltpu.VMEM)
    return pl.pallas_call(
        functools.partial(image_kernel, count_x, count_z),
        in_specs=[pl.BlockSpec(memory_space=pltpu.SMEM), vmem],
        out_specs=vmem,
        out_shape=jax.ShapeDtypeStruct((4, TILE, count_x * 2 * LANES), jnp.float32),
        compiler_params=pltpu.CompilerParams(vmem_limit_bytes=40 * 1024 * 1024),
        name="compose",
    )(order, codes)


def per_device(fields, breakpoints, tf_color, tf_opacity, depth_order, live_rows):
    count_x, count_z = lax.axis_size("bx"), lax.axis_size("bz")
    live = live_rows.reshape(2)
    tf = (breakpoints, tf_color, tf_opacity, live)
    rim = rims(fields)
    behind = lax.ppermute(rim, "bx", [(i, i + 1) for i in range(count_x - 1)])
    codes = with_edges(fields.shape[1], *tf, behind, rim, brick(*tf, fields))
    codes = lax.all_to_all(codes, ("bx", "bz"), split_axis=0, concat_axis=0, tiled=True)
    return compose(depth_order, codes, count_x, count_z)


def solution(mesh):
    return jax.shard_map(
        per_device,
        mesh=mesh,
        in_specs=(P(None, "bz", None, "bx"), P(), P(), P(), P(), P("bx", "bz", None)),
        out_specs=P(None, ("bx", "bz"), None),
        check_vma=False,
    )
```
